32 devices in a mesh: dp: 4 (over z), ctx: 8 (over y, x, core).
Axes of the slice: x: 2, y: 2, z: 4, core: 2. Of those that a mesh axis runs over, the one named last changes fastest.
Arguments:
- inputs: bfloat16 [4, 4096, 4096], P('dp', 'ctx'), may hold values from -6 to 6
- qkv_weight: bfloat16 [4096, 768], P('ctx'), may hold values from -0.09375 to 0.09375
- queries: bfloat16 [4, 4096, 512], P('dp', 'ctx'), may hold values from -6 to 6
- keys_values: bfloat16 [4, 4096, 256], P('dp', 'ctx'), may hold values from -6 to 6
- out_grad: bfloat16 [4, 4096, 512], P('dp', 'ctx'), may hold values from -6 to 6
- lengths: int32 [4, 16], P('dp'), may hold values from 1 to 1536, as said below
Outputs:
- grad_queries: bfloat16 [4, 4096, 512], P('dp', 'ctx')
- grad_kv: bfloat16 [4, 4096, 256], P('dp', 'ctx')
- grad_inputs: bfloat16 [4, 4096, 4096], P('dp', 'ctx')
- grad_weight: bfloat16 [4096, 768], P('ctx')
The draws below stay inside these ranges and needn't reach their ends.
Inputs may be any that keep to these rules, and one draw needn't show every extreme that they name: Each row's lengths sum to 4096; the first is 1, the second exactly 1536, none longer.
All inputs are finite; a program needn't handle non-finite values.
Results may differ from the reference program's by a relative error of at most 0.0074.
Values may be sent and summed in bfloat16 or wider, within the bound.
No kernel may reach another device: no remote copies, remote signals or barrier semaphores. Data moves between devices by JAX's collectives and lax.ppermute only.
A program may use at most 128 MiB of HBM per device.

```python
import jax
import jax.numpy as jnp
from jax import lax

D = 4096
HEADS = 4
HD = 128
NDOC = 16
ROW = 4096
MOST = 1536
C = 768
N_DP = 4


def draw_queries(key, part):
    own_key = jax.random.fold_in(key, 11)
    shape_full = (N_DP, ROW, HEADS * HD)
    base = jnp.clip(jax.random.normal(own_key, shape_full, jnp.float32), -6.0, 6.0)
    return base.astype(jnp.bfloat16)


def draw_keys_values(key, part):
    own_key = jax.random.fold_in(key, 12)
    shape_full = (N_DP, ROW, 2 * HD)
    base = jnp.clip(jax.random.normal(own_key, shape_full, jnp.float32), -6.0, 6.0)
    return base.astype(jnp.bfloat16)


def draw_lengths(key, part):
    own_key = jax.random.fold_in(key, 13)
    weights = jax.random.randint(own_key, (N_DP, NDOC - 2), 1, 10).astype(jnp.int32)
    spare_units = ROW - MOST - 1 - (NDOC - 2)
    total_weight = jnp.sum(weights, axis=1, keepdims=True)
    extra_units = jnp.minimum(spare_units * weights // total_weight, MOST - 1)
    leftover = spare_units - jnp.sum(extra_units, axis=1)
    columns = []
    for index in range(NDOC - 2):
        room_left = MOST - 1 - extra_units[:, index]
        added = jnp.minimum(leftover, room_left)
        columns.append(extra_units[:, index] + added + 1)
        leftover = leftover - added
    remainder = jnp.stack(columns, axis=1)
    first_doc = jnp.ones((N_DP, 1), jnp.int32)
    second_doc = jnp.full((N_DP, 1), MOST, jnp.int32)
    return jnp.concatenate([first_doc, second_doc, remainder], axis=1).astype(jnp.int32)


def spiked(values, stream_key, source, target, parts, factor):
    def block_of(position):
        return (jnp.arange(values.shape[position]) // (values.shape[position] // parts)).reshape((-1,) + (1,) * (values.ndim - 1 - position))

    first = jax.random.permutation(stream_key, parts)[block_of(target)]
    other_side = (block_of(target) + parts // 2) % parts
    return jnp.where((block_of(source) == first) | (block_of(source) == other_side), factor * values, values)


def shard_levels(key, dims, shards, smallest, largest):
    factor_of, own = 1.0, jax.random.fold_in(key, 6)
    for position, parts in shards:
        draws = jnp.exp(jax.random.uniform(jax.random.fold_in(own, position), (parts,), jnp.float32, smallest / len(shards), largest / len(shards)))
        factor_of = factor_of * jnp.repeat(draws, dims[position] // parts).reshape([-1 if axis == position else 1 for axis in range(len(dims))])
    return factor_of


def noise(key, extent, width, limit, shards=(), kind=jnp.bfloat16):
    array = jax.random.normal(key, extent, jnp.float32) * width
    if len(shards) > 0:
        array = shard_levels(key, extent, shards, -0.22, 0.18) * array
    return jnp.clip(array, min=-limit, max=limit).astype(kind)


def gaussian_with(key, dims, width, most, shards, heavy, kind=jnp.bfloat16):
    array = width * jax.random.normal(key, dims, jnp.float32)
    if shards:
        array = array * shard_levels(key, dims, shards, -0.22, 0.18)
    return jnp.clip(spiked(array, jax.random.fold_in(key, 3), *heavy), -most, most).astype(kind)


def setup_inputs(seed: int = 0) -> dict:
    splits = jax.random.split(jax.random.key(seed), 7)
    inputs = gaussian_with(splits[0], (N_DP, ROW, D), 1.0, 6.0, ((0, 4), (1, 8)), (1, 2, 8, 2.0))
    qkv_weight = noise(splits[1], (D, C), D ** -0.5, 0.09375, ((0, 8),))
    queries = draw_queries(jax.random.fold_in(splits[6], 71), 0)
    keys_values = draw_keys_values(jax.random.fold_in(splits[6], 71), 0)
    out_grad = noise(splits[4], (N_DP, ROW, HEADS * HD), 1.0, 6.0, ((0, 4), (1, 8)))
    lengths = draw_lengths(jax.random.fold_in(splits[6], 71), 0)
    return dict(inputs=inputs, qkv_weight=qkv_weight, queries=queries, keys_values=keys_values, out_grad=out_grad, lengths=lengths)


def row_grads(queries_row, kv_row, grad_row, lengths_row):
    scaling = HD ** -0.5
    doc_ends = jnp.cumsum(lengths_row)
    positions = jnp.arange(ROW, dtype=jnp.int32)
    doc_ids = jnp.sum((positions[:, None] >= doc_ends[None, :]).astype(jnp.int32), axis=1)
    q_all = queries_row.astype(jnp.float32).reshape(ROW, HEADS, HD)
    g_all = grad_row.astype(jnp.float32).reshape(ROW, HEADS, HD)
    kv_all = kv_row.astype(jnp.float32)
    q_block = min(512, ROW)
    k_window = min(ROW, MOST + q_block)

    def step_block(carried, block_index):
        q_start = (block_index * q_block).astype(jnp.int32)
        k_start = jnp.clip(q_start + q_block - k_window, 0, ROW - k_window).astype(jnp.int32)
        query_rows = lax.dynamic_slice_in_dim(q_all, q_start, q_block, 0)
        grad_rows = lax.dynamic_slice_in_dim(g_all, q_start, q_block, 0)
        kv_rows = lax.dynamic_slice_in_dim(kv_all, k_start, k_window, 0)
        keys_part = kv_rows[:, :HD]
        values_part = kv_rows[:, HD:]
        q_pos = q_start + jnp.arange(q_block, dtype=jnp.int32)
        k_pos = k_start + jnp.arange(k_window, dtype=jnp.int32)
        q_doc = lax.dynamic_slice_in_dim(doc_ids, q_start, q_block, 0)
        k_doc = lax.dynamic_slice_in_dim(doc_ids, k_start, k_window, 0)
        allowed = (q_doc[:, None] == k_doc[None, :]) & (k_pos[None, :] <= q_pos[:, None])
        scores = jnp.einsum("thd,kd->htk", query_rows, keys_part) * scaling
        masked = jnp.where(allowed[None], scores, -jnp.inf)
        top_score = jnp.max(masked, axis=2)
        totals = jnp.sum(jnp.where(allowed[None], jnp.exp(scores - top_score[:, :, None]), 0.0), axis=2)
        lse = top_score + jnp.log(totals)
        probs = jnp.where(allowed[None], jnp.exp(scores - lse[:, :, None]), 0.0)
        dprobs = jnp.einsum("thd,kd->htk", grad_rows, values_part)
        delta = jnp.sum(probs * dprobs, axis=2)
        dscores = probs * (dprobs - delta[:, :, None])
        probs_low = lax.optimization_barrier(probs.astype(jnp.bfloat16)).astype(jnp.float32)
        dscores_low = lax.optimization_barrier(dscores.astype(jnp.bfloat16)).astype(jnp.float32)
        dq_rows = (scaling * jnp.einsum("htk,kd->thd", dscores_low, keys_part)).astype(jnp.bfloat16)
        dk_rows = scaling * jnp.einsum("htk,thd->kd", dscores_low, query_rows)
        dv_rows = jnp.einsum("htk,thd->kd", probs_low, grad_rows)
        updated = lax.dynamic_slice_in_dim(carried, k_start, k_window, 0) + jnp.concatenate([dk_rows, dv_rows], axis=1)
        carried = lax.dynamic_update_slice_in_dim(carried, updated, k_start, 0)
        return carried, dq_rows.reshape(q_block, HEADS * HD)

    start_kv = jnp.zeros((ROW, 2 * HD), jnp.float32)
    block_ids = jnp.arange(ROW // q_block, dtype=jnp.int32)
    kv_total, dq_blocks = lax.scan(step_block, start_kv, block_ids)
    return dq_blocks.reshape(ROW, HEADS * HD), kv_total.astype(jnp.bfloat16)


def row_entry(packed):
    return row_grads(packed[0], packed[1], packed[2], packed[3])


def input_entry(grad_qkv_row, qkv_weight):
    return jnp.dot(grad_qkv_row, qkv_weight.T, preferred_element_type=jnp.float32).astype(jnp.bfloat16)


def reference(inputs, qkv_weight, queries, keys_values, out_grad, lengths):
    grad_queries, grad_kv = lax.map(row_entry, (queries, keys_values, out_grad, lengths))
    grad_qkv = jnp.concatenate([grad_queries, grad_kv], axis=2)
    grad_inputs = lax.map(lambda grad_qkv_row: input_entry(grad_qkv_row, qkv_weight), grad_qkv)

    def weight_step(carried, packed):
        return carried + jnp.dot(packed[0].T, packed[1], preferred_element_type=jnp.float32), None

    weight_sum = lax.scan(weight_step, jnp.zeros((D, C), jnp.float32), (inputs, grad_qkv))[0]
    return grad_queries, grad_kv, grad_inputs, weight_sum.astype(jnp.bfloat16)
```

```python
import functools

import jax
import jax.numpy as jnp
from jax import lax
from jax.experimental import pallas as pl
from jax.experimental.pallas import tpu as pltpu
from jax.sharding import PartitionSpec as P

MOST = 1536
NEG_FILL = -1e30
LOG2E = 1.4426950408889634
KEY_STEP = 256
Q_STEP = 128


def nt_dot(a, b):
    return lax.dot_general(a, b, (((1,), (1,)), ((), ())), preferred_element_type=jnp.float32)


def nn_dot(a, b):
    return lax.dot_general(a, b, (((1,), (0,)), ((), ())), preferred_element_type=jnp.float32)


def attention_kernel(
    idx_ref, len_ref, q_ref, g_ref, own_ref, d2_ref, r_ref, x_ref,
    gq_ref, gqt_ref, own_out, d2_out, r_out, x_out,
    kv_scr, kt_scr, s_scr, dp_scr, acc_scr,
):
    rows = q_ref.shape[0]
    hd = kv_scr.shape[1] // 2
    heads = q_ref.shape[1] // hd
    wide = heads * Q_STEP
    scaling = hd ** (-0.5)
    index = idx_ref[0]
    parity = lax.rem(index, 2)
    base = (index - 3) * rows
    r_off = pl.multiple_of((1 - parity) * 2 * rows, rows)
    x_off = pl.multiple_of(parity * 2 * rows, rows)
    kv_scr[pl.ds(r_off, rows), :] = r_ref[...]
    kv_scr[pl.ds(x_off, rows), :] = x_ref[...]
    kv_scr[rows : 2 * rows, :] = d2_ref[...]
    kv_scr[3 * rows :, :] = own_ref[...]
    for slot in range(4):
        part = slice(slot * rows, (slot + 1) * rows)
        kt_scr[:, part] = kv_scr[part, :hd].T
    acc_scr[...] = jnp.zeros_like(acc_scr)
    ends = []
    total = -base
    for j in range(len_ref.shape[1]):
        ends.append(total)
        total = total + len_ref[0, j]

    for tile in range(rows // Q_STEP):
        q_rows = slice(tile * Q_STEP, (tile + 1) * Q_STEP)
        first = 3 * rows + tile * Q_STEP
        q_pos = first + (lax.broadcasted_iota(jnp.int32, (1, wide), 1) & (Q_STEP - 1))
        doc_start = jnp.full((1, wide), ends[0], jnp.int32)
        least = ends[0]
        for end in ends[1:]:
            doc_start = jnp.where(q_pos >= end, end, doc_start)
            least = jnp.where(first >= end, end, least)
        q_cat = jnp.concatenate([q_ref[q_rows, h * hd : (h + 1) * hd] for h in range(heads)], axis=0)
        g_cat = jnp.concatenate([g_ref[q_rows, h * hd : (h + 1) * hd] for h in range(heads)], axis=0)
        begin = jnp.maximum(least, 0) // KEY_STEP
        stop = -(-(first + Q_STEP) // KEY_STEP)

        def scores_step(c, top):
            at = pl.ds(pl.multiple_of(c * KEY_STEP, KEY_STEP), KEY_STEP)
            s = nt_dot(kv_scr[at, :hd], q_cat)
            k_pos = c * KEY_STEP + lax.broadcasted_iota(jnp.int32, (KEY_STEP, wide), 0)
            s = jnp.where((k_pos >= doc_start) & (k_pos <= q_pos), s, NEG_FILL)
            s_scr[at, :] = s
            dp_scr[at, :] = nt_dot(kv_scr[at, hd:], g_cat)
            return jnp.maximum(top, jnp.max(s, axis=0, keepdims=True))

        top = lax.fori_loop(begin, stop, scores_step, jnp.full((1, wide), NEG_FILL, jnp.float32))

        def sums_step(c, carried):
            at = pl.ds(pl.multiple_of(c * KEY_STEP, KEY_STEP), KEY_STEP)
            e = jnp.exp2((s_scr[at, :] - top) * (scaling * LOG2E))
            s_scr[at, :] = e
            return (
                carried[0] + jnp.sum(e, axis=0, keepdims=True),
                carried[1] + jnp.sum(e * dp_scr[at, :], axis=0, keepdims=True),
            )

        zero = jnp.zeros((1, wide), jnp.float32)
        norm, dot = lax.fori_loop(begin, stop, sums_step, (zero, zero))
        inverse = 1.0 / norm
        delta = dot * inverse

        def grads_step(c, dq):
            at = pl.ds(pl.multiple_of(c * KEY_STEP, KEY_STEP), KEY_STEP)
            p = s_scr[at, :] * inverse
            ds_low = (p * (dp_scr[at, :] - delta)).astype(jnp.bfloat16)
            p_low = p.astype(jnp.bfloat16)
            acc_scr[at, :hd] += nn_dot(ds_low, q_cat)
            acc_scr[at, hd:] += nn_dot(p_low, g_cat)
            return dq + nn_dot(kt_scr[:, at], ds_low)

        dq = lax.fori_loop(begin, stop, grads_step, jnp.zeros((hd, wide), jnp.float32)) * scaling
        for h in range(heads):
            piece = dq[:, h * Q_STEP : (h + 1) * Q_STEP]
            gqt_ref[h * hd : (h + 1) * hd, q_rows] = piece.astype(jnp.bfloat16)
            gq_ref[q_rows, h * hd : (h + 1) * hd] = piece.T.astype(jnp.bfloat16)

    def put(out, at):
        out[:, :hd] = (acc_scr[at, :hd] * scaling).astype(out.dtype)
        out[:, hd:] = acc_scr[at, hd:].astype(out.dtype)

    put(r_out, pl.ds(r_off, rows))
    put(x_out, pl.ds(x_off, rows))
    put(d2_out, slice(rows, 2 * rows))
    put(own_out, slice(3 * rows, 4 * rows))


def attention(index, lengths, q, g, own, d2, r, x):
    rows, width = q.shape
    both = own.shape[1]
    hd = both // 2
    wide = width // hd * Q_STEP
    vmem = pl.BlockSpec(memory_space=pltpu.VMEM)
    smem = pl.BlockSpec(memory_space=pltpu.SMEM)
    return pl.pallas_call(
        attention_kernel,
        name="attention",
        out_shape=(
            jax.ShapeDtypeStruct((rows, width), jnp.bfloat16),
            jax.ShapeDtypeStruct((width, rows), jnp.bfloat16),
            jax.ShapeDtypeStruct((rows, both), jnp.float32),
            jax.ShapeDtypeStruct((rows, both), jnp.float32),
            jax.ShapeDtypeStruct((rows, both), jnp.float32),
            jax.ShapeDtypeStruct((rows, both), jnp.bfloat16),
        ),
        in_specs=[smem, smem] + [vmem] * 6,
        out_specs=[vmem] * 6,
        scratch_shapes=[
            pltpu.VMEM((4 * rows, both), jnp.bfloat16),
            pltpu.VMEM((hd, 4 * rows), jnp.bfloat16),
            pltpu.VMEM((4 * rows, wide), jnp.float32),
            pltpu.VMEM((4 * rows, wide), jnp.float32),
            pltpu.VMEM((4 * rows, both), jnp.float32),
        ],
        compiler_params=pltpu.CompilerParams(vmem_limit_bytes=40 * 2**20),
        cost_estimate=pl.CostEstimate(flops=6 * 10**9, bytes_accessed=6 * 2**20, transcendentals=4 * 2**20),
    )(index, lengths, q, g, own, d2, r, x)


def weight_kernel(places, gt_ref, gt_other, x_ref, x_other, own_out, *outs):
    k = pl.program_id(0)
    total = nn_dot(gt_ref[...], x_ref[...]) + nn_dot(gt_other[...], x_other[...])

    @pl.when(k == 0)
    def _():
        own_out[...] = total

    for turn, out in enumerate(outs):
        @pl.when(k == turn + 1)
        def _(out=out):
            out[...] = total.astype(out.dtype)


def weight_partials(places, gt, gt_other, x, x_other, block):
    cols, rows = gt.shape
    chips = x_other.shape[1] // block
    whole = lambda k, s: (0, 0)
    return pl.pallas_call(
        weight_kernel,
        name="weight_partials",
        out_shape=[jax.ShapeDtypeStruct((cols, block), jnp.float32)]
        + [jax.ShapeDtypeStruct((cols, block), jnp.bfloat16)] * (chips - 1),
        grid_spec=pltpu.PrefetchScalarGridSpec(
            num_scalar_prefetch=1,
            grid=(chips,),
            in_specs=[
                pl.BlockSpec((cols, rows), whole),
                pl.BlockSpec((cols, rows), whole),
                pl.BlockSpec((rows, block), lambda k, s: (0, (s[0] ^ k) * 2 + s[1])),
                pl.BlockSpec((rows, block), lambda k, s: (0, s[0] ^ k)),
            ],
            out_specs=[pl.BlockSpec((cols, block), whole)] * chips,
        ),
        compiler_params=pltpu.CompilerParams(vmem_limit_bytes=40 * 2**20),
        cost_estimate=pl.CostEstimate(
            flops=4 * cols * rows * block * chips, bytes_accessed=8 * 2**20, transcendentals=0
        ),
    )(places, gt, gt_other, x, x_other)


def input_kernel(places, gq_ref, gkv_ref, *refs):
    out_ref = refs[-1]
    k = pl.program_id(0)
    q_cols = gq_ref.shape[1]
    for turn, w_ref in enumerate(refs[:-1]):
        @pl.when(k == turn)
        def _(w_ref=w_ref):
            out_ref[...] = (
                nt_dot(gq_ref[...], w_ref[:, :q_cols]) + nt_dot(gkv_ref[...], w_ref[:, q_cols:])
            ).astype(out_ref.dtype)


def input_grad(places, gq, gkv, blocks):
    rows = gq.shape[0]
    block, cols = blocks[0].shape
    count = len(blocks)
    whole = lambda k, s: (0, 0)
    return pl.pallas_call(
        input_kernel,
        name="input_grad",
        out_shape=jax.ShapeDtypeStruct((rows, block * count), jnp.bfloat16),
        grid_spec=pltpu.PrefetchScalarGridSpec(
            num_scalar_prefetch=1,
            grid=(count,),
            in_specs=[pl.BlockSpec(gq.shape, whole), pl.BlockSpec(gkv.shape, whole)]
            + [pl.BlockSpec((block, cols), whole)] * count,
            out_specs=pl.BlockSpec((rows, block), lambda k, s: (0, (s[0] * 2 + s[1]) ^ k)),
        ),
        compiler_params=pltpu.CompilerParams(vmem_limit_bytes=40 * 2**20),
        cost_estimate=pl.CostEstimate(
            flops=2 * rows * cols * block * count, bytes_accessed=11 * 2**20, transcendentals=0
        ),
    )(places, gq, gkv, *blocks)


def flipped(array, bits):
    size = lax.axis_size("ctx")
    return lax.ppermute(array, "ctx", [(i, i ^ bits) for i in range(size)])


def tree_sum(part):
    z = lax.axis_index("dp")
    first = lax.ppermute(part.astype(jnp.bfloat16), "dp", [(0, 1), (3, 2)])
    half = lax.optimization_barrier((part + first.astype(jnp.float32)).astype(jnp.bfloat16))
    other = lax.ppermute(half, "dp", [(1, 2), (2, 1)])
    full = (half.astype(jnp.float32) + other.astype(jnp.float32)).astype(jnp.bfloat16)
    back = lax.ppermute(full, "dp", [(1, 0), (2, 3)])
    return jnp.where((z == 1) | (z == 2), full, back)


def per_device(inputs, qkv_weight, queries, keys_values, out_grad, lengths):
    f32, bf16 = jnp.float32, jnp.bfloat16
    size = lax.axis_size("ctx")
    planes = lax.axis_size("dp")
    index = lax.axis_index("ctx")
    core = index % 2
    chip = index // 2
    rows = queries.shape[1]
    assert MOST == 3 * rows
    own = keys_values[0]
    by_two = [(i, i + 2) for i in range(size - 2)]
    mixed = [(i, i + 1) for i in range(0, size, 2)] + [(i, i + 3) for i in range(1, size - 3, 2)]
    back = lambda pairs: [(b, a) for a, b in pairs]
    small = size == 8 and planes == 4
    block = qkv_weight.shape[0]

    d2 = lax.ppermute(own, "ctx", by_two)
    x = lax.ppermute(own, "ctx", mixed)
    r = flipped(d2, 1)
    x_local = inputs[0]
    if small:
        x_pairs = x_local.reshape(rows, size // 2, 2, block)
        x_send = lax.dynamic_index_in_dim(x_pairs, 1 - core, 2, keepdims=False).reshape(rows, -1)
        x_other = flipped(x_send, 1)
        w_parts = [qkv_weight] + [flipped(qkv_weight, bits) for bits in (2, 4, 6)]
        w_other = [flipped(w, 1) for w in w_parts]
        w_blocks = [w for pair in zip(w_parts, w_other) for w in pair]
    else:
        w_full = lax.all_gather(qkv_weight, "ctx", axis=0, tiled=True)

    gq, gqt, kv_own, kv_d2, kv_r, kv_x = attention(
        index.reshape(1), lengths, queries[0], out_grad[0], own, d2, r, x
    )
    kv_d2 = (kv_d2 + flipped(kv_r, 1)).astype(bf16)
    from_two = lax.ppermute(kv_d2, "ctx", back(by_two))
    from_x = lax.ppermute(kv_x, "ctx", back(mixed))
    gkv = (kv_own + from_two.astype(f32) + from_x.astype(f32)).astype(bf16)

    if small:
        places = jnp.stack([chip, core])

        def reduced(gt):
            mine, *others = weight_partials(places, gt, flipped(gt, 1), x_local, x_other, block)
            for bits, other in zip((2, 4, 6), others):
                mine = mine + flipped(other, bits).astype(f32)
            return tree_sum(mine)

        weight_q = reduced(gqt)
        weight_kv = reduced(gkv.T)
        weight_sum = jnp.concatenate([weight_q, weight_kv], axis=0).T
        grad_in = input_grad(places, gq, gkv, w_blocks)
    else:
        grad_qkv = jnp.concatenate([gq, gkv], axis=1)
        grad_in = nt_dot(grad_qkv, w_full).astype(bf16)
        partial = lax.dot_general(
            x_local, grad_qkv, (((0,), (0,)), ((), ())), preferred_element_type=f32
        )
        shard = lax.psum_scatter(partial, "ctx", scatter_dimension=0, tiled=True)
        weight_sum = lax.psum(shard, "dp").astype(bf16)
    return (gq[None], gkv[None], grad_in[None], weight_sum)


def solution(mesh):
    placed = (
        P("dp", "ctx", None),
        P("ctx", None),
        P("dp", "ctx", None),
        P("dp", "ctx", None),
        P("dp", "ctx", None),
        P("dp", None),
    )
    return jax.shard_map(
        per_device,
        mesh=mesh,
        in_specs=placed,
        out_specs=(
            P("dp", "ctx", None),
            P("dp", "ctx", None),
            P("dp", "ctx", None),
            P("ctx", None),
        ),
        check_vma=False,
    )
```

```python
import functools

import jax
import jax.numpy as jnp
from jax import lax
from jax.experimental import pallas as pl
from jax.experimental.pallas import tpu as pltpu
from jax.sharding import PartitionSpec as P

MOST = 1536
NEG_FILL = -1e30
LOG2E = 1.4426950408889634
KEY_STEP = 256
Q_STEP = 128


def nt_dot(a, b):
    return lax.dot_general(a, b, (((1,), (1,)), ((), ())), preferred_element_type=jnp.float32)


def nn_dot(a, b):
    return lax.dot_general(a, b, (((1,), (0,)), ((), ())), preferred_element_type=jnp.float32)


def attention_kernel(
    idx_ref, len_ref, q_ref, g_ref, own_ref, d2_ref, r_ref, x_ref,
    gq_ref, gqt_ref, own_out, d2_out, r_out, x_out,
    kv_scr, kt_scr, s_scr, dp_scr, acc_scr,
):
    rows = q_ref.shape[0]
    hd = kv_scr.shape[1] // 2
    heads = q_ref.shape[1] // hd
    wide = heads * Q_STEP
    scaling = hd ** (-0.5)
    index = idx_ref[0]
    parity = lax.rem(index, 2)
    base = (index - 3) * rows
    r_off = pl.multiple_of((1 - parity) * 2 * rows, rows)
    x_off = pl.multiple_of(parity * 2 * rows, rows)
    kv_scr[pl.ds(r_off, rows), :] = r_ref[...]
    kv_scr[pl.ds(x_off, rows), :] = x_ref[...]
    kv_scr[rows : 2 * rows, :] = d2_ref[...]
    kv_scr[3 * rows :, :] = own_ref[...]
    for slot in range(4):
        part = slice(slot * rows, (slot + 1) * rows)
        kt_scr[:, part] = kv_scr[part, :hd].T
    acc_scr[...] = jnp.zeros_like(acc_scr)
    ends = []
    total = -base
    for j in range(len_ref.shape[1]):
        ends.append(total)
        total = total + len_ref[0, j]

    for tile in range(rows // Q_STEP):
        q_rows = slice(tile * Q_STEP, (tile + 1) * Q_STEP)
        first = 3 * rows + tile * Q_STEP
        q_pos = first + (lax.broadcasted_iota(jnp.int32, (1, wide), 1) & (Q_STEP - 1))
        doc_start = jnp.full((1, wide), ends[0], jnp.int32)
        least = ends[0]
        for end in ends[1:]:
            doc_start = jnp.where(q_pos >= end, end, doc_start)
            least = jnp.where(first >= end, end, least)
        q_cat = jnp.concatenate([q_ref[q_rows, h * hd : (h + 1) * hd] for h in range(heads)], axis=0)
        g_cat = jnp.concatenate([g_ref[q_rows, h * hd : (h + 1) * hd] for h in range(heads)], axis=0)
        begin = jnp.maximum(least, 0) // KEY_STEP
        stop = -(-(first + Q_STEP) // KEY_STEP)

        def scores_step(c, top):
            at = pl.ds(pl.multiple_of(c * KEY_STEP, KEY_STEP), KEY_STEP)
            s = nt_dot(kv_scr[at, :hd], q_cat)
            k_pos = c * KEY_STEP + lax.broadcasted_iota(jnp.int32, (KEY_STEP, wide), 0)
            s = jnp.where((k_pos >= doc_start) & (k_pos <= q_pos), s, NEG_FILL)
            s_scr[at, :] = s
            dp_scr[at, :] = nt_dot(kv_scr[at, hd:], g_cat)
            return jnp.maximum(top, jnp.max(s, axis=0, keepdims=True))

        top = lax.fori_loop(begin, stop, scores_step, jnp.full((1, wide), NEG_FILL, jnp.float32))

        def sums_step(c, carried):
            at = pl.ds(pl.multiple_of(c * KEY_STEP, KEY_STEP), KEY_STEP)
            e = jnp.exp2((s_scr[at, :] - top) * (scaling * LOG2E))
            s_scr[at, :] = e
            return (
                carried[0] + jnp.sum(e, axis=0, keepdims=True),
                carried[1] + jnp.sum(e * dp_scr[at, :], axis=0, keepdims=True),
            )

        zero = jnp.zeros((1, wide), jnp.float32)
        norm, dot = lax.fori_loop(begin, stop, sums_step, (zero, zero))
        inverse = 1.0 / norm
        delta = dot * inverse

        def grads_step(c, dq):
            at = pl.ds(pl.multiple_of(c * KEY_STEP, KEY_STEP), KEY_STEP)
            p = s_scr[at, :] * inverse
            ds_low = (p * (dp_scr[at, :] - delta)).astype(jnp.bfloat16)
            p_low = p.astype(jnp.bfloat16)
            acc_scr[at, :hd] += nn_dot(ds_low, q_cat)
            acc_scr[at, hd:] += nn_dot(p_low, g_cat)
            return dq + nn_dot(kt_scr[:, at], ds_low)

        dq = lax.fori_loop(begin, stop, grads_step, jnp.zeros((hd, wide), jnp.float32)) * scaling
        for h in range(heads):
            piece = dq[:, h * Q_STEP : (h + 1) * Q_STEP]
            gqt_ref[h * hd : (h + 1) * hd, q_rows] = piece.astype(jnp.bfloat16)
            gq_ref[q_rows, h * hd : (h + 1) * hd] = piece.T.astype(jnp.bfloat16)

    def put(out, at):
        out[:, :hd] = (acc_scr[at, :hd] * scaling).astype(out.dtype)
        out[:, hd:] = acc_scr[at, hd:].astype(out.dtype)

    put(r_out, pl.ds(r_off, rows))
    put(x_out, pl.ds(x_off, rows))
    put(d2_out, slice(rows, 2 * rows))
    put(own_out, slice(3 * rows, 4 * rows))


def attention(index, lengths, q, g, own, d2, r, x):
    rows, width = q.shape
    both = own.shape[1]
    hd = both // 2
    wide = width // hd * Q_STEP
    vmem = pl.BlockSpec(memory_space=pltpu.VMEM)
    smem = pl.BlockSpec(memory_space=pltpu.SMEM)
    return pl.pallas_call(
        attention_kernel,
        name="attention",
        out_shape=(
            jax.ShapeDtypeStruct((rows, width), jnp.bfloat16),
            jax.ShapeDtypeStruct((width, rows), jnp.bfloat16),
            jax.ShapeDtypeStruct((rows, both), jnp.float32),
            jax.ShapeDtypeStruct((rows, both), jnp.float32),
            jax.ShapeDtypeStruct((rows, both), jnp.float32),
            jax.ShapeDtypeStruct((rows, both), jnp.bfloat16),
        ),
        in_specs=[smem, smem] + [vmem] * 6,
        out_specs=[vmem] * 6,
        scratch_shapes=[
            pltpu.VMEM((4 * rows, both), jnp.bfloat16),
            pltpu.VMEM((hd, 4 * rows), jnp.bfloat16),
            pltpu.VMEM((4 * rows, wide), jnp.float32),
            pltpu.VMEM((4 * rows, wide), jnp.float32),
            pltpu.VMEM((4 * rows, both), jnp.float32),
        ],
        compiler_params=pltpu.CompilerParams(vmem_limit_bytes=28 * 2**20),
        cost_estimate=pl.CostEstimate(flops=12 * 10**9, bytes_accessed=6 * 2**20, transcendentals=4 * 2**20),
    )(index, lengths, q, g, own, d2, r, x)


def weight_kernel(places, gt_ref, gt_other, x_ref, x_other, own_out, *outs):
    k = pl.program_id(0)
    total = nn_dot(gt_ref[...], x_ref[...]) + nn_dot(gt_other[...], x_other[...])

    @pl.when(k == 0)
    def _():
        own_out[...] = total

    for turn, out in enumerate(outs):
        @pl.when(k == turn + 1)
        def _(out=out):
            out[...] = total.astype(out.dtype)


def weight_partials(places, gt, gt_other, x, x_other, block):
    cols, rows = gt.shape
    chips = x_other.shape[1] // block // 2
    whole = lambda k, s: (0, 0)
    return pl.pallas_call(
        weight_kernel,
        name="weight_partials",
        out_shape=[jax.ShapeDtypeStruct((cols, block), jnp.float32)]
        + [jax.ShapeDtypeStruct((cols, block), jnp.bfloat16)] * (chips - 1),
        grid_spec=pltpu.PrefetchScalarGridSpec(
            num_scalar_prefetch=1,
            grid=(chips,),
            in_specs=[
                pl.BlockSpec((cols, rows), whole),
                pl.BlockSpec((cols, rows), whole),
                pl.BlockSpec((rows, block), lambda k, s: (0, (s[0] ^ k) * 2 + s[1])),
                pl.BlockSpec((rows, block), lambda k, s: (0, (s[0] ^ k) * 2 + s[1])),
            ],
            out_specs=[pl.BlockSpec((cols, block), whole)] * chips,
        ),
        compiler_params=pltpu.CompilerParams(vmem_limit_bytes=40 * 2**20),
        cost_estimate=pl.CostEstimate(
            flops=4 * cols * rows * block * chips, bytes_accessed=8 * 2**20, transcendentals=0
        ),
    )(places, gt, gt_other, x, x_other)


def input_kernel(places, gq_ref, gkv_ref, *refs):
    out_ref = refs[-1]
    k = pl.program_id(0)
    q_cols = gq_ref.shape[1]
    for turn, w_ref in enumerate(refs[:-1]):
        @pl.when(k == turn)
        def _(w_ref=w_ref):
            out_ref[...] = (
                nt_dot(gq_ref[...], w_ref[:, :q_cols]) + nt_dot(gkv_ref[...], w_ref[:, q_cols:])
            ).astype(out_ref.dtype)


def input_grad(places, gq, gkv, blocks):
    rows = gq.shape[0]
    block, cols = blocks[0].shape
    count = len(blocks)
    whole = lambda k, s: (0, 0)
    return pl.pallas_call(
        input_kernel,
        name="input_grad",
        out_shape=jax.ShapeDtypeStruct((rows, block * count), jnp.bfloat16),
        grid_spec=pltpu.PrefetchScalarGridSpec(
            num_scalar_prefetch=1,
            grid=(count,),
            in_specs=[pl.BlockSpec(gq.shape, whole), pl.BlockSpec(gkv.shape, whole)]
            + [pl.BlockSpec((block, cols), whole)] * count,
            out_specs=pl.BlockSpec((rows, block), lambda k, s: (0, (s[0] * 2 + s[1]) ^ k)),
        ),
        compiler_params=pltpu.CompilerParams(vmem_limit_bytes=40 * 2**20),
        cost_estimate=pl.CostEstimate(
            flops=2 * rows * cols * block * count, bytes_accessed=11 * 2**20, transcendentals=0
        ),
    )(places, gq, gkv, *blocks)


def finish_kernel(own_ref, two_ref, x_ref, out_ref, out_t_ref):
    total = own_ref[...] + two_ref[...].astype(jnp.float32) + x_ref[...].astype(jnp.float32)
    out_ref[...] = total.astype(out_ref.dtype)
    out_t_ref[...] = total.T.astype(out_t_ref.dtype)


def finish_kv(own, from_two, from_x):
    rows, cols = own.shape
    return pl.pallas_call(
        finish_kernel,
        name="finish_kv",
        out_shape=(
            jax.ShapeDtypeStruct((rows, cols), jnp.bfloat16),
            jax.ShapeDtypeStruct((cols, rows), jnp.bfloat16),
        ),
        cost_estimate=pl.CostEstimate(flops=4 * rows * cols, bytes_accessed=2**21, transcendentals=0),
    )(own, from_two, from_x)


def quarters_kernel(z_ref, own_ref, a_ref, b_ref, c_ref, mine_out, *outs):
    z = z_ref[0]
    quarter = mine_out.shape[0]
    for k, out in enumerate((mine_out, *outs)):
        at = pl.ds(pl.multiple_of((z ^ k) * quarter, quarter), quarter)
        total = own_ref[at, :]
        for ref in (a_ref, b_ref, c_ref):
            total = total + ref[at, :].astype(jnp.float32)
        out[...] = total.astype(out.dtype)


def quarters_of(z, own, others):
    rows, cols = own.shape
    piece = (rows // 4, cols)
    vmem = pl.BlockSpec(own.shape, lambda i: (0, 0))
    out = pl.BlockSpec(piece, lambda i: (0, 0))
    return pl.pallas_call(
        quarters_kernel,
        name="quarters",
        out_shape=[jax.ShapeDtypeStruct(piece, jnp.float32)] + [jax.ShapeDtypeStruct(piece, jnp.bfloat16)] * 3,
        grid=(1,),
        in_specs=[pl.BlockSpec(memory_space=pltpu.SMEM)] + [vmem] * 4,
        out_specs=[out] * 4,
        cost_estimate=pl.CostEstimate(flops=4 * rows * cols, bytes_accessed=2**21, transcendentals=0),
    )(z, own, *others)


def joined_kernel(z_ref, *refs):
    z = z_ref[0]
    count = (len(refs) - 2) // 4
    out_ref, scr = refs[-2:]
    start = 0
    for part in range(count):
        pieces = refs[4 * part : 4 * part + 4]
        quarter = pieces[0].shape[0]
        for k, piece in enumerate(pieces):
            scr[pl.ds(pl.multiple_of(start + (z ^ k) * quarter, quarter), quarter), :] = piece[...]
        start += 4 * quarter
    out_ref[...] = scr[...].T


def joined(z, parts):
    pieces = [piece for part in parts for piece in part]
    cols = pieces[0].shape[1]
    rows = sum(piece.shape[0] for piece in pieces)
    return pl.pallas_call(
        joined_kernel,
        name="joined",
        out_shape=jax.ShapeDtypeStruct((cols, rows), jnp.bfloat16),
        grid=(1,),
        in_specs=[pl.BlockSpec(memory_space=pltpu.SMEM)]
        + [pl.BlockSpec(piece.shape, lambda i: (0, 0)) for piece in pieces],
        out_specs=pl.BlockSpec((cols, rows), lambda i: (0, 0)),
        scratch_shapes=[pltpu.VMEM((rows, cols), jnp.bfloat16)],
        cost_estimate=pl.CostEstimate(flops=rows * cols, bytes_accessed=2**21, transcendentals=0),
    )(z, *pieces)


def flipped(array, bits, axis="ctx"):
    return lax.ppermute(array, axis, [(i, i ^ bits) for i in range(lax.axis_size(axis))])


def tied(array, *after):
    return lax.optimization_barrier((array, *after))[0]


def per_device(inputs, qkv_weight, queries, keys_values, out_grad, lengths):
    f32, bf16 = jnp.float32, jnp.bfloat16
    size = lax.axis_size("ctx")
    planes = lax.axis_size("dp")
    index = lax.axis_index("ctx")
    rows = queries.shape[1]
    assert MOST == 3 * rows
    own = keys_values[0]
    by_two = [(i, i + 2) for i in range(size - 2)]
    mixed = [(i, i + 1) for i in range(0, size, 2)] + [(i, i + 3) for i in range(1, size - 3, 2)]
    back = lambda pairs: [(b, a) for a, b in pairs]
    small = size == 8 and planes == 4
    block = qkv_weight.shape[0]
    x_local = inputs[0]

    d2 = lax.ppermute(own, "ctx", by_two)
    x = lax.ppermute(own, "ctx", mixed)
    r = flipped(d2, 1)
    if small:
        w_own = tied(qkv_weight, d2, x)
        w_parts = [w_own] + [flipped(w_own, bits) for bits in (2, 4, 6)]
        x_other = flipped(tied(x_local, r), 1)
    else:
        w_full = lax.all_gather(qkv_weight, "ctx", axis=0, tiled=True)

    gq, gqt, kv_own, kv_d2, kv_r, kv_x = attention(
        index.reshape(1), lengths, queries[0], out_grad[0], own, d2, r, x
    )
    kv_d2 = (kv_d2 + flipped(kv_r, 1)).astype(bf16)
    from_two = lax.ppermute(kv_d2, "ctx", back(by_two))
    from_x = lax.ppermute(kv_x, "ctx", back(mixed))
    gkv, gkvt = finish_kv(kv_own, from_two, from_x)

    if small:
        places = jnp.stack([index // 2, index % 2])
        z = lax.axis_index("dp").reshape(1)

        def reduced(gt, *after):
            gt_other = tied(flipped(gt, 1), *after)
            mine, *others = weight_partials(places, gt, gt_other, x_local, x_other, block)
            others = [flipped(other, bits) for bits, other in zip((2, 4, 6), others)]
            mine, *pieces = quarters_of(z, mine, others)
            for k, piece in enumerate(pieces):
                mine = mine + flipped(piece, k + 1, "dp").astype(f32)
            mine = mine.astype(bf16)
            return [mine] + [flipped(mine, k, "dp") for k in (1, 2, 3)]

        parts = [reduced(gqt, *w_parts), reduced(gkvt)]
        weight_sum = joined(z, parts)
        w_blocks = [w for part in w_parts for w in (part, flipped(part, 1))]
        grad_in = input_grad(places, gq, gkv, w_blocks)
    else:
        grad_qkv = jnp.concatenate([gq, gkv], axis=1)
        grad_in = nt_dot(grad_qkv, w_full).astype(bf16)
        partial = lax.dot_general(
            x_local, grad_qkv, (((0,), (0,)), ((), ())), preferred_element_type=f32
        )
        shard = lax.psum_scatter(partial, "ctx", scatter_dimension=0, tiled=True)
        weight_sum = lax.psum(shard, "dp").astype(bf16)
    return (gq[None], gkv[None], grad_in[None], weight_sum)


def solution(mesh):
    placed = (
        P("dp", "ctx", None),
        P("ctx", None),
        P("dp", "ctx", None),
        P("dp", "ctx", None),
        P("dp", "ctx", None),
        P("dp", None),
    )
    return jax.shard_map(
        per_device,
        mesh=mesh,
        in_specs=placed,
        out_specs=(
            P("dp", "ctx", None),
            P("dp", "ctx", None),
            P("dp", "ctx", None),
            P("ctx", None),
        ),
        check_vma=False,
    )
```

```python
import functools

import jax
import jax.numpy as jnp
from jax import lax
from jax.experimental import pallas as pl
from jax.experimental.pallas import tpu as pltpu
from jax.sharding import PartitionSpec as P

MOST = 1536
NEG_FILL = -1e30
LOG2E = 1.4426950408889634
KEY_STEP = 256
Q_STEP = 128


def nt_dot(a, b):
    return lax.dot_general(a, b, (((1,), (1,)), ((), ())), preferred_element_type=jnp.float32)


def nn_dot(a, b):
    return lax.dot_general(a, b, (((1,), (0,)), ((), ())), preferred_element_type=jnp.float32)


def attention_kernel(
    idx_ref, len_ref, q_ref, g_ref, own_ref, d2_ref, r_ref, x_ref,
    gq_ref, gqt_ref, own_out, d2_out, r_out, x_out,
    kv_scr, kt_scr, s_scr, dp_scr, acc_scr,
):
    rows = q_ref.shape[0]
    hd = kv_scr.shape[1] // 2
    heads = q_ref.shape[1] // hd
    wide = heads * Q_STEP
    scaling = hd ** (-0.5)
    index = idx_ref[0]
    parity = lax.rem(index, 2)
    base = (index - 3) * rows
    r_off = pl.multiple_of((1 - parity) * 2 * rows, rows)
    x_off = pl.multiple_of(parity * 2 * rows, rows)
    kv_scr[pl.ds(r_off, rows), :] = r_ref[...]
    kv_scr[pl.ds(x_off, rows), :] = x_ref[...]
    kv_scr[rows : 2 * rows, :] = d2_ref[...]
    kv_scr[3 * rows :, :] = own_ref[...]
    for slot in range(4):
        part = slice(slot * rows, (slot + 1) * rows)
        kt_scr[:, part] = kv_scr[part, :hd].T
    acc_scr[...] = jnp.zeros_like(acc_scr)
    ends = []
    total = -base
    for j in range(len_ref.shape[1]):
        ends.append(total)
        total = total + len_ref[0, j]

    for tile in range(rows // Q_STEP):
        q_rows = slice(tile * Q_STEP, (tile + 1) * Q_STEP)
        first = 3 * rows + tile * Q_STEP
        q_pos = first + (lax.broadcasted_iota(jnp.int32, (1, wide), 1) & (Q_STEP - 1))
        doc_start = jnp.full((1, wide), ends[0], jnp.int32)
        least = ends[0]
        for end in ends[1:]:
            doc_start = jnp.where(q_pos >= end, end, doc_start)
            least = jnp.where(first >= end, end, least)
        q_cat = jnp.concatenate([q_ref[q_rows, h * hd : (h + 1) * hd] for h in range(heads)], axis=0)
        g_cat = jnp.concatenate([g_ref[q_rows, h * hd : (h + 1) * hd] for h in range(heads)], axis=0)
        begin = jnp.maximum(least, 0) // KEY_STEP
        stop = -(-(first + Q_STEP) // KEY_STEP)

        def scores_step(c, top):
            at = pl.ds(pl.multiple_of(c * KEY_STEP, KEY_STEP), KEY_STEP)
            s = nt_dot(kv_scr[at, :hd], q_cat)
            k_pos = c * KEY_STEP + lax.broadcasted_iota(jnp.int32, (KEY_STEP, wide), 0)
            s = jnp.where((k_pos >= doc_start) & (k_pos <= q_pos), s, NEG_FILL)
            s_scr[at, :] = s
            dp_scr[at, :] = nt_dot(kv_scr[at, hd:], g_cat)
            return jnp.maximum(top, jnp.max(s, axis=0, keepdims=True))

        top = lax.fori_loop(begin, stop, scores_step, jnp.full((1, wide), NEG_FILL, jnp.float32))

        def sums_step(c, carried):
            at = pl.ds(pl.multiple_of(c * KEY_STEP, KEY_STEP), KEY_STEP)
            e = jnp.exp2((s_scr[at, :] - top) * (scaling * LOG2E))
            s_scr[at, :] = e
            return (
                carried[0] + jnp.sum(e, axis=0, keepdims=True),
                carried[1] + jnp.sum(e * dp_scr[at, :], axis=0, keepdims=True),
            )

        zero = jnp.zeros((1, wide), jnp.float32)
        norm, dot = lax.fori_loop(begin, stop, sums_step, (zero, zero))
        inverse = 1.0 / norm
        delta = dot * inverse

        def grads_step(c, dq):
            at = pl.ds(pl.multiple_of(c * KEY_STEP, KEY_STEP), KEY_STEP)
            p = s_scr[at, :] * inverse
            ds_low = (p * (dp_scr[at, :] - delta)).astype(jnp.bfloat16)
            p_low = p.astype(jnp.bfloat16)
            acc_scr[at, :hd] += nn_dot(ds_low, q_cat)
            acc_scr[at, hd:] += nn_dot(p_low, g_cat)
            return dq + nn_dot(kt_scr[:, at], ds_low)

        dq = lax.fori_loop(begin, stop, grads_step, jnp.zeros((hd, wide), jnp.float32)) * scaling
        for h in range(heads):
            piece = dq[:, h * Q_STEP : (h + 1) * Q_STEP]
            gqt_ref[h * hd : (h + 1) * hd, q_rows] = piece.astype(jnp.bfloat16)
            gq_ref[q_rows, h * hd : (h + 1) * hd] = piece.T.astype(jnp.bfloat16)

    def put(out, at):
        out[:, :hd] = (acc_scr[at, :hd] * scaling).astype(out.dtype)
        out[:, hd:] = acc_scr[at, hd:].astype(out.dtype)

    put(r_out, pl.ds(r_off, rows))
    put(x_out, pl.ds(x_off, rows))
    put(d2_out, slice(rows, 2 * rows))
    put(own_out, slice(3 * rows, 4 * rows))


def attention(index, lengths, q, g, own, d2, r, x):
    rows, width = q.shape
    both = own.shape[1]
    hd = both // 2
    wide = width // hd * Q_STEP
    whole = lambda shape: pl.BlockSpec(shape, lambda i: (0, 0))
    smem = pl.BlockSpec(memory_space=pltpu.SMEM)
    return pl.pallas_call(
        attention_kernel,
        name="attention",
        out_shape=(
            jax.ShapeDtypeStruct((rows, width), jnp.bfloat16),
            jax.ShapeDtypeStruct((width, rows), jnp.bfloat16),
            jax.ShapeDtypeStruct((rows, both), jnp.float32),
            jax.ShapeDtypeStruct((rows, both), jnp.float32),
            jax.ShapeDtypeStruct((rows, both), jnp.float32),
            jax.ShapeDtypeStruct((rows, both), jnp.bfloat16),
        ),
        grid=(1,),
        in_specs=[smem, smem] + [whole((rows, width))] * 2 + [whole((rows, both))] * 4,
        out_specs=[whole((rows, width)), whole((width, rows))] + [whole((rows, both))] * 4,
        scratch_shapes=[
            pltpu.VMEM((4 * rows, both), jnp.bfloat16),
            pltpu.VMEM((hd, 4 * rows), jnp.bfloat16),
            pltpu.VMEM((4 * rows, wide), jnp.float32),
            pltpu.VMEM((4 * rows, wide), jnp.float32),
            pltpu.VMEM((4 * rows, both), jnp.float32),
        ],
        compiler_params=pltpu.CompilerParams(vmem_limit_bytes=58 * 2**20),
        cost_estimate=pl.CostEstimate(flops=12 * 10**9, bytes_accessed=6 * 2**20, transcendentals=4 * 2**20),
    )(index, lengths, q, g, own, d2, r, x)


def weight_kernel(places, gt_ref, gt_other, x_ref, x_other, own_out, *outs):
    k = pl.program_id(0)
    total = nn_dot(gt_ref[...], x_ref[...]) + nn_dot(gt_other[...], x_other[...])

    @pl.when(k == 0)
    def _():
        own_out[...] = total

    for turn, out in enumerate(outs):
        @pl.when(k == turn + 1)
        def _(out=out):
            out[...] = total.astype(out.dtype)


def weight_partials(places, gt, gt_other, x, x_other, block):
    cols, rows = gt.shape
    chips = x_other.shape[1] // block // 2
    whole = lambda k, s: (0, 0)
    return pl.pallas_call(
        weight_kernel,
        name="weight_partials",
        out_shape=[jax.ShapeDtypeStruct((cols, block), jnp.float32)]
        + [jax.ShapeDtypeStruct((cols, block), jnp.bfloat16)] * (chips - 1),
        grid_spec=pltpu.PrefetchScalarGridSpec(
            num_scalar_prefetch=1,
            grid=(chips,),
            in_specs=[
                pl.BlockSpec((cols, rows), whole),
                pl.BlockSpec((cols, rows), whole),
                pl.BlockSpec((rows, block), lambda k, s: (0, (s[0] ^ k) * 2 + s[1])),
                pl.BlockSpec((rows, block), lambda k, s: (0, (s[0] ^ k) * 2 + s[1])),
            ],
            out_specs=[pl.BlockSpec((cols, block), whole)] * chips,
        ),
        compiler_params=pltpu.CompilerParams(vmem_limit_bytes=58 * 2**20),
        cost_estimate=pl.CostEstimate(
            flops=4 * cols * rows * block * chips, bytes_accessed=8 * 2**20, transcendentals=0
        ),
    )(places, gt, gt_other, x, x_other)


def input_kernel(places, gq_ref, gkv_ref, *refs, count):
    out_ref = refs[-1]
    k = pl.program_id(0)
    q_cols = gq_ref.shape[1]
    for turn, w_ref in enumerate(refs[:count]):
        @pl.when(k == turn)
        def _(w_ref=w_ref):
            out_ref[...] = (
                nt_dot(gq_ref[...], w_ref[:, :q_cols]) + nt_dot(gkv_ref[...], w_ref[:, q_cols:])
            ).astype(out_ref.dtype)


def input_grad(places, gq, gkv, blocks, start, earlier=None):
    rows = gq.shape[0]
    block, cols = blocks[0].shape
    count = len(blocks)
    total = lax.axis_size("ctx") * block
    whole = lambda k, s: (0, 0)
    before = [] if earlier is None else [earlier]
    return pl.pallas_call(
        functools.partial(input_kernel, count=count),
        name="input_grad",
        out_shape=jax.ShapeDtypeStruct((rows, total), jnp.bfloat16),
        grid_spec=pltpu.PrefetchScalarGridSpec(
            num_scalar_prefetch=1,
            grid=(count,),
            in_specs=[pl.BlockSpec(gq.shape, whole), pl.BlockSpec(gkv.shape, whole)]
            + [pl.BlockSpec((block, cols), whole)] * count
            + [pl.BlockSpec(memory_space=pl.ANY)] * len(before),
            out_specs=pl.BlockSpec((rows, block), lambda k, s: (0, (s[0] * 2 + s[1]) ^ (start + k))),
        ),
        input_output_aliases={3 + count: 0} if before else {},
        compiler_params=pltpu.CompilerParams(vmem_limit_bytes=58 * 2**20),
        cost_estimate=pl.CostEstimate(
            flops=2 * rows * cols * block * count, bytes_accessed=11 * 2**20, transcendentals=0
        ),
    )(places, gq, gkv, *blocks, *before)


def finish_kernel(own_ref, two_ref, x_ref, out_ref, out_t_ref):
    total = own_ref[...] + two_ref[...].astype(jnp.float32) + x_ref[...].astype(jnp.float32)
    out_ref[...] = total.astype(out_ref.dtype)
    out_t_ref[...] = total.T.astype(out_t_ref.dtype)


def finish_kv(own, from_two, from_x):
    rows, cols = own.shape
    return pl.pallas_call(
        finish_kernel,
        name="finish_kv",
        out_shape=(
            jax.ShapeDtypeStruct((rows, cols), jnp.bfloat16),
            jax.ShapeDtypeStruct((cols, rows), jnp.bfloat16),
        ),
        cost_estimate=pl.CostEstimate(flops=4 * rows * cols, bytes_accessed=2**21, transcendentals=0),
    )(own, from_two, from_x)


def quarters_kernel(z_ref, own_ref, a_ref, b_ref, c_ref, mine_out, *outs):
    z = z_ref[0]
    quarter = mine_out.shape[0]
    for k, out in enumerate((mine_out, *outs)):
        at = pl.ds(pl.multiple_of((z ^ k) * quarter, quarter), quarter)
        total = own_ref[at, :]
        for ref in (a_ref, b_ref, c_ref):
            total = total + ref[at, :].astype(jnp.float32)
        out[...] = total.astype(out.dtype)


def quarters_of(z, own, others):
    rows, cols = own.shape
    piece = (rows // 4, cols)
    vmem = pl.BlockSpec(own.shape, lambda i: (0, 0))
    out = pl.BlockSpec(piece, lambda i: (0, 0))
    return pl.pallas_call(
        quarters_kernel,
        name="quarters",
        out_shape=[jax.ShapeDtypeStruct(piece, jnp.float32)] + [jax.ShapeDtypeStruct(piece, jnp.bfloat16)] * 3,
        grid=(1,),
        in_specs=[pl.BlockSpec(memory_space=pltpu.SMEM)] + [vmem] * 4,
        out_specs=[out] * 4,
        cost_estimate=pl.CostEstimate(flops=4 * rows * cols, bytes_accessed=2**21, transcendentals=0),
    )(z, own, *others)


def joined_kernel(z_ref, *refs):
    z = z_ref[0]
    count = (len(refs) - 2) // 4
    out_ref, scr = refs[-2:]
    start = 0
    for part in range(count):
        pieces = refs[4 * part : 4 * part + 4]
        quarter = pieces[0].shape[0]
        for k, piece in enumerate(pieces):
            scr[pl.ds(pl.multiple_of(start + (z ^ k) * quarter, quarter), quarter), :] = piece[...]
        start += 4 * quarter
    out_ref[...] = scr[...].T


def joined(z, parts):
    pieces = [piece for part in parts for piece in part]
    cols = pieces[0].shape[1]
    rows = sum(piece.shape[0] for piece in pieces)
    return pl.pallas_call(
        joined_kernel,
        name="joined",
        out_shape=jax.ShapeDtypeStruct((cols, rows), jnp.bfloat16),
        grid=(1,),
        in_specs=[pl.BlockSpec(memory_space=pltpu.SMEM)]
        + [pl.BlockSpec(piece.shape, lambda i: (0, 0)) for piece in pieces],
        out_specs=pl.BlockSpec((cols, rows), lambda i: (0, 0)),
        scratch_shapes=[pltpu.VMEM((rows, cols), jnp.bfloat16)],
        cost_estimate=pl.CostEstimate(flops=rows * cols, bytes_accessed=2**21, transcendentals=0),
    )(z, *pieces)


def flipped(array, bits, axis="ctx"):
    return lax.ppermute(array, axis, [(i, i ^ bits) for i in range(lax.axis_size(axis))])


def together(*arrays):
    return lax.optimization_barrier(arrays)


def per_device(inputs, qkv_weight, queries, keys_values, out_grad, lengths):
    f32, bf16 = jnp.float32, jnp.bfloat16
    size = lax.axis_size("ctx")
    planes = lax.axis_size("dp")
    index = lax.axis_index("ctx")
    rows = queries.shape[1]
    assert MOST == 3 * rows
    own = keys_values[0]
    by_two = [(i, i + 2) for i in range(size - 2)]
    mixed = [(i, i + 1) for i in range(0, size, 2)] + [(i, i + 3) for i in range(1, size - 3, 2)]
    back = lambda pairs: [(b, a) for a, b in pairs]
    small = size == 8 and planes == 4
    block = qkv_weight.shape[0]
    x_local = inputs[0]

    d2 = lax.ppermute(own, "ctx", by_two)
    x = lax.ppermute(own, "ctx", mixed)
    d2, x = lax.optimization_barrier((d2, x))
    r = flipped(d2, 1)
    if small:
        w_own, x_in, r = lax.optimization_barrier((qkv_weight, x_local, r))
        w_x, w_y = flipped(w_own, 2), flipped(w_own, 4)
        x_other = flipped(x_in, 1)
    else:
        w_full = lax.all_gather(qkv_weight, "ctx", axis=0, tiled=True)

    grads = attention(index.reshape(1), lengths, queries[0], out_grad[0], own, d2, r, x)
    if small:
        *grads, w_x, w_y, x_other = lax.optimization_barrier((*grads, w_x, w_y, x_other))
    gq, gqt, kv_own, kv_d2, kv_r, kv_x = grads
    kv_d2 = (kv_d2 + flipped(kv_r, 1)).astype(bf16)
    from_two = lax.ppermute(kv_d2, "ctx", back(by_two))
    from_x = lax.ppermute(kv_x, "ctx", back(mixed))

    if small:
        places = jnp.stack([index // 2, index % 2])
        z = lax.axis_index("dp").reshape(1)

        def partials(gt):
            return weight_partials(places, gt, flipped(gt, 1), x_local, x_other, block)

        def sent(others):
            return [flipped(other, bits) for bits, other in zip((2, 4, 6), others)]

        def crossed(pieces):
            return [flipped(piece, k + 1, "dp") for k, piece in enumerate(pieces)]

        def added(mine, pieces):
            for piece in pieces:
                mine = mine + piece.astype(f32)
            return mine.astype(bf16)

        q_own, *q_others = partials(gqt)
        kv_own, q_own, w_own, w_x, w_y = together(kv_own, q_own, w_own, w_x, w_y)
        gkv, gkvt = finish_kv(kv_own, from_two, from_x)
        q_others = sent(q_others)
        kv_part, *kv_others = partials(gkvt)
        w_blocks = [w for part in (w_own, w_x, w_y) for w in (part, flipped(part, 1))]
        kv_others = sent(kv_others)
        grad_in = input_grad(places, gq, gkv, w_blocks, 0)
        *q_others, grad_in = together(*q_others, grad_in)
        q_own, *q_pieces = quarters_of(z, q_own, q_others)
        q_pieces = crossed(q_pieces)
        *q_pieces, a, b, c, w_own = together(*q_pieces, *kv_others, w_own)
        kv_part, *kv_pieces = quarters_of(z, kv_part, (a, b, c))
        w_d = flipped(w_own, 6)
        q_mine = added(q_own, q_pieces)
        q_all = crossed([q_mine] * 3)
        kv_pieces = crossed(kv_pieces)
        *kv_pieces, a, b, c, w_d = together(*kv_pieces, *q_all, w_d)
        kv_mine = added(kv_part, kv_pieces)
        kv_all = crossed([kv_mine] * 3)
        grad_in = input_grad(places, gq, gkv, (w_d, flipped(w_d, 1)), 6, grad_in)
        *kv_all, grad_in = together(*kv_all, grad_in)
        weight_sum = joined(z, [(q_mine, a, b, c), (kv_mine, *kv_all)])
    else:
        gkv, _ = finish_kv(kv_own, from_two, from_x)
        grad_qkv = jnp.concatenate([gq, gkv], axis=1)
        grad_in = nt_dot(grad_qkv, w_full).astype(bf16)
        partial = lax.dot_general(
            x_local, grad_qkv, (((0,), (0,)), ((), ())), preferred_element_type=f32
        )
        shard = lax.psum_scatter(partial, "ctx", scatter_dimension=0, tiled=True)
        weight_sum = lax.psum(shard, "dp").astype(bf16)
    return (gq[None], gkv[None], grad_in[None], weight_sum)


def solution(mesh):
    placed = (
        P("dp", "ctx", None),
        P("ctx", None),
        P("dp", "ctx", None),
        P("dp", "ctx", None),
        P("dp", "ctx", None),
        P("dp", None),
    )
    return jax.shard_map(
        per_device,
        mesh=mesh,
        in_specs=placed,
        out_specs=(
            P("dp", "ctx", None),
            P("dp", "ctx", None),
            P("dp", "ctx", None),
            P("ctx", None),
        ),
        check_vma=False,
    )
```

```python
import functools

import jax
import jax.numpy as jnp
from jax import lax
from jax.experimental import pallas as pl
from jax.experimental.pallas import tpu as pltpu
from jax.sharding import PartitionSpec as P

MOST = 1536
NEG_FILL = -1e30
LOG2E = 1.4426950408889634
KEY_STEP = 512
Q_STEP = 256


def nt_dot(a, b):
    return lax.dot_general(a, b, (((1,), (1,)), ((), ())), preferred_element_type=jnp.float32)


def nn_dot(a, b):
    return lax.dot_general(a, b, (((1,), (0,)), ((), ())), preferred_element_type=jnp.float32)


def attention_kernel(
    idx_ref, len_ref, q_ref, g_ref, own_ref, d2_ref, r_ref, x_ref,
    gq_ref, gqt_ref, own_out, d2_out, r_out, x_out,
    kv_scr, kt_scr, s_scr, dp_scr, acc_scr,
):
    rows = q_ref.shape[0]
    hd = kv_scr.shape[1] // 2
    heads = q_ref.shape[1] // hd
    wide = heads * Q_STEP
    scaling = hd ** (-0.5)
    index = idx_ref[0]
    parity = lax.rem(index, 2)
    base = (index - 3) * rows
    r_off = pl.multiple_of((1 - parity) * 2 * rows, rows)
    x_off = pl.multiple_of(parity * 2 * rows, rows)
    kv_scr[pl.ds(r_off, rows), :] = r_ref[...]
    kv_scr[pl.ds(x_off, rows), :] = x_ref[...]
    kv_scr[rows : 2 * rows, :] = d2_ref[...]
    kv_scr[3 * rows :, :] = own_ref[...]
    for slot in range(4):
        part = slice(slot * rows, (slot + 1) * rows)
        kt_scr[:, part] = kv_scr[part, :hd].T
    acc_scr[...] = jnp.zeros_like(acc_scr)
    ends = []
    total = -base
    for j in range(len_ref.shape[1]):
        ends.append(total)
        total = total + len_ref[0, j]

    for tile in range(rows // Q_STEP):
        q_rows = slice(tile * Q_STEP, (tile + 1) * Q_STEP)
        first = 3 * rows + tile * Q_STEP
        q_pos = first + (lax.broadcasted_iota(jnp.int32, (1, wide), 1) & (Q_STEP - 1))
        doc_start = jnp.full((1, wide), ends[0], jnp.int32)
        least = ends[0]
        for end in ends[1:]:
            doc_start = jnp.where(q_pos >= end, end, doc_start)
            least = jnp.where(first >= end, end, least)
        q_cat = jnp.concatenate([q_ref[q_rows, h * hd : (h + 1) * hd] for h in range(heads)], axis=0)
        g_cat = jnp.concatenate([g_ref[q_rows, h * hd : (h + 1) * hd] for h in range(heads)], axis=0)
        begin = jnp.maximum(least, 0) // KEY_STEP
        stop = -(-(first + Q_STEP) // KEY_STEP)

        def scores_step(c, carried):
            top, norm, dot = carried
            at = pl.ds(pl.multiple_of(c * KEY_STEP, KEY_STEP), KEY_STEP)
            s = nt_dot(kv_scr[at, :hd], q_cat) * (scaling * LOG2E)
            k_pos = c * KEY_STEP + lax.broadcasted_iota(jnp.int32, (KEY_STEP, wide), 0)
            s = jnp.where((k_pos >= doc_start) & (k_pos <= q_pos), s, NEG_FILL)
            s_scr[at, :] = s
            dp = nt_dot(kv_scr[at, hd:], g_cat)
            dp_scr[at, :] = dp
            s = s.reshape(KEY_STEP // 8, 8, wide)
            above = jnp.maximum(top, jnp.max(s, axis=0))
            shrink = jnp.exp2(top - above)
            e = jnp.exp2(s - above[None])
            norm = norm * shrink + jnp.sum(e, axis=0)
            dot = dot * shrink + jnp.sum(e * dp.reshape(KEY_STEP // 8, 8, wide), axis=0)
            return above, norm, dot

        zero = jnp.zeros((8, wide), jnp.float32)
        tops, norms, dots = lax.fori_loop(
            begin, stop, scores_step, (jnp.full((8, wide), NEG_FILL, jnp.float32), zero, zero)
        )
        top = jnp.max(tops, axis=0, keepdims=True)
        shrink = jnp.exp2(tops - top)
        norm = jnp.sum(norms * shrink, axis=0, keepdims=True)
        delta = jnp.sum(dots * shrink, axis=0, keepdims=True) / norm
        lse = top + jnp.log2(norm)

        def grads_step(c, dq):
            at = pl.ds(pl.multiple_of(c * KEY_STEP, KEY_STEP), KEY_STEP)
            p = jnp.exp2(s_scr[at, :] - lse)
            ds_low = (p * (dp_scr[at, :] - delta)).astype(jnp.bfloat16)
            p_low = p.astype(jnp.bfloat16)
            acc_scr[at, :hd] += nn_dot(ds_low, q_cat)
            acc_scr[at, hd:] += nn_dot(p_low, g_cat)
            return dq + nn_dot(kt_scr[:, at], ds_low)

        dq = lax.fori_loop(begin, stop, grads_step, jnp.zeros((hd, wide), jnp.float32)) * scaling
        for h in range(heads):
            piece = dq[:, h * Q_STEP : (h + 1) * Q_STEP]
            gqt_ref[h * hd : (h + 1) * hd, q_rows] = piece.astype(jnp.bfloat16)
            gq_ref[q_rows, h * hd : (h + 1) * hd] = piece.T.astype(jnp.bfloat16)

    def put(out, at):
        out[:, :hd] = (acc_scr[at, :hd] * scaling).astype(out.dtype)
        out[:, hd:] = acc_scr[at, hd:].astype(out.dtype)

    put(r_out, pl.ds(r_off, rows))
    put(x_out, pl.ds(x_off, rows))
    put(d2_out, slice(rows, 2 * rows))
    put(own_out, slice(3 * rows, 4 * rows))


def attention(index, lengths, q, g, own, d2, r, x):
    rows, width = q.shape
    both = own.shape[1]
    hd = both // 2
    wide = width // hd * Q_STEP
    whole = lambda shape: pl.BlockSpec(shape, lambda i: (0, 0))
    smem = pl.BlockSpec(memory_space=pltpu.SMEM)
    return pl.pallas_call(
        attention_kernel,
        name="attention",
        out_shape=(
            jax.ShapeDtypeStruct((rows, width), jnp.bfloat16),
            jax.ShapeDtypeStruct((width, rows), jnp.bfloat16),
            jax.ShapeDtypeStruct((rows, both), jnp.float32),
            jax.ShapeDtypeStruct((rows, both), jnp.float32),
            jax.ShapeDtypeStruct((rows, both), jnp.float32),
            jax.ShapeDtypeStruct((rows, both), jnp.bfloat16),
        ),
        grid=(1,),
        in_specs=[smem, smem] + [whole((rows, width))] * 2 + [whole((rows, both))] * 4,
        out_specs=[whole((rows, width)), whole((width, rows))] + [whole((rows, both))] * 4,
        scratch_shapes=[
            pltpu.VMEM((4 * rows, both), jnp.bfloat16),
            pltpu.VMEM((hd, 4 * rows), jnp.bfloat16),
            pltpu.VMEM((4 * rows, wide), jnp.float32),
            pltpu.VMEM((4 * rows, wide), jnp.float32),
            pltpu.VMEM((4 * rows, both), jnp.float32),
        ],
        compiler_params=pltpu.CompilerParams(vmem_limit_bytes=58 * 2**20),
        cost_estimate=pl.CostEstimate(flops=12 * 10**9, bytes_accessed=6 * 2**20, transcendentals=4 * 2**20),
    )(index, lengths, q, g, own, d2, r, x)


def weight_kernel(places, gt_ref, gt_other, x_ref, x_other, own_out, keep_out, to_x, to_y):
    k = pl.program_id(0)
    half = gt_ref.shape[0] // 2
    upper, lower = slice(0, half), slice(half, 2 * half)
    total = nn_dot(gt_ref[...], x_ref[...]) + nn_dot(gt_other[...], x_other[...])
    low = total.astype(jnp.bfloat16)

    @pl.when(k == 3)
    def _():
        own_out[...] = total

    @pl.when(k == 1)
    def _():
        to_x[upper, :] = low[upper, :]
        keep_out[lower, :] = low[lower, :]

    @pl.when(k == 2)
    def _():
        keep_out[upper, :] = low[upper, :]
        to_y[upper, :] = low[lower, :]

    @pl.when(k == 0)
    def _():
        to_x[lower, :] = low[upper, :]
        to_y[lower, :] = low[lower, :]


def weight_partials(places, gt, gt_other, x, x_other, block):
    cols, rows = gt.shape
    chips = x_other.shape[1] // block // 2
    whole = lambda k, s: (0, 0)
    strip = pl.BlockSpec((rows, block), lambda k, s: (0, (s[0] ^ s[2 + k]) * 2 + s[1]))
    return pl.pallas_call(
        weight_kernel,
        name="weight_partials",
        out_shape=[jax.ShapeDtypeStruct((cols, block), jnp.float32)]
        + [jax.ShapeDtypeStruct((cols, block), jnp.bfloat16)] * 3,
        grid_spec=pltpu.PrefetchScalarGridSpec(
            num_scalar_prefetch=1,
            grid=(chips,),
            in_specs=[pl.BlockSpec((cols, rows), whole)] * 2 + [strip] * 2,
            out_specs=[pl.BlockSpec((cols, block), whole)] * 4,
        ),
        compiler_params=pltpu.CompilerParams(vmem_limit_bytes=58 * 2**20),
        cost_estimate=pl.CostEstimate(
            flops=4 * cols * rows * block * chips, bytes_accessed=8 * 2**20, transcendentals=0
        ),
    )(places, gt, gt_other, x, x_other)


def middle_kernel(own_ref, keep_ref, from_x, from_y, own_out, next_x, next_y):
    f32 = jnp.float32
    half = own_ref.shape[0] // 2
    upper, lower = slice(0, half), slice(half, 2 * half)
    own_out[upper, :] = own_ref[upper, :] + from_x[upper, :].astype(f32)
    own_out[lower, :] = own_ref[lower, :] + from_y[upper, :].astype(f32)
    next_y[...] = (keep_ref[upper, :].astype(f32) + from_x[lower, :].astype(f32)).astype(next_y.dtype)
    next_x[...] = (keep_ref[lower, :].astype(f32) + from_y[lower, :].astype(f32)).astype(next_x.dtype)


def middle(own, keep, from_x, from_y):
    rows, cols = own.shape
    half = jax.ShapeDtypeStruct((rows // 2, cols), jnp.bfloat16)
    return pl.pallas_call(
        middle_kernel,
        name="middle",
        out_shape=[jax.ShapeDtypeStruct(own.shape, jnp.float32), half, half],
        cost_estimate=pl.CostEstimate(flops=4 * rows * cols, bytes_accessed=2**21, transcendentals=0),
    )(own, keep, from_x, from_y)


def input_kernel(places, gq_ref, gkv_ref, *refs, count):
    out_ref = refs[-1]
    k = pl.program_id(0)
    q_cols = gq_ref.shape[1]
    for turn, w_ref in enumerate(refs[:count]):
        @pl.when(k == turn)
        def _(w_ref=w_ref):
            out_ref[...] = (
                nt_dot(gq_ref[...], w_ref[:, :q_cols]) + nt_dot(gkv_ref[...], w_ref[:, q_cols:])
            ).astype(out_ref.dtype)


def input_grad(places, gq, gkv, blocks, start, earlier=None):
    rows = gq.shape[0]
    block, cols = blocks[0].shape
    count = len(blocks)
    total = lax.axis_size("ctx") * block
    whole = lambda k, s: (0, 0)
    before = [] if earlier is None else [earlier]
    return pl.pallas_call(
        functools.partial(input_kernel, count=count),
        name="input_grad",
        out_shape=jax.ShapeDtypeStruct((rows, total), jnp.bfloat16),
        grid_spec=pltpu.PrefetchScalarGridSpec(
            num_scalar_prefetch=1,
            grid=(count,),
            in_specs=[pl.BlockSpec(gq.shape, whole), pl.BlockSpec(gkv.shape, whole)]
            + [pl.BlockSpec((block, cols), whole)] * count
            + [pl.BlockSpec(memory_space=pl.ANY)] * len(before),
            out_specs=pl.BlockSpec((rows, block), lambda k, s: (0, (s[0] * 2 + s[1]) ^ (start + k))),
        ),
        input_output_aliases={3 + count: 0} if before else {},
        compiler_params=pltpu.CompilerParams(vmem_limit_bytes=58 * 2**20),
        cost_estimate=pl.CostEstimate(
            flops=2 * rows * cols * block * count, bytes_accessed=11 * 2**20, transcendentals=0
        ),
    )(places, gq, gkv, *blocks, *before)


def finish_kernel(own_ref, two_ref, x_ref, out_ref, out_t_ref):
    total = own_ref[...] + two_ref[...].astype(jnp.float32) + x_ref[...].astype(jnp.float32)
    out_ref[...] = total.astype(out_ref.dtype)
    out_t_ref[...] = total.T.astype(out_t_ref.dtype)


def finish_kv(own, from_two, from_x):
    rows, cols = own.shape
    return pl.pallas_call(
        finish_kernel,
        name="finish_kv",
        out_shape=(
            jax.ShapeDtypeStruct((rows, cols), jnp.bfloat16),
            jax.ShapeDtypeStruct((cols, rows), jnp.bfloat16),
        ),
        cost_estimate=pl.CostEstimate(flops=4 * rows * cols, bytes_accessed=2**21, transcendentals=0),
    )(own, from_two, from_x)


def quarters_kernel(z_ref, own_ref, x_ref, y_ref, mine_out, *outs):
    z = z_ref[0]
    quarter = mine_out.shape[0]
    for k, out in enumerate((mine_out, *outs)):
        place = z ^ k
        at = pl.ds(pl.multiple_of(place * quarter, quarter), quarter)
        half = pl.ds(pl.multiple_of(lax.rem(place, 2) * quarter, quarter), quarter)
        add = jnp.where(place < 2, y_ref[half, :].astype(jnp.float32), x_ref[half, :].astype(jnp.float32))
        out[...] = (own_ref[at, :] + add).astype(out.dtype)


def quarters_of(z, own, from_x, from_y):
    rows, cols = own.shape
    piece = (rows // 4, cols)
    whole = lambda i: (0, 0)
    out = pl.BlockSpec(piece, whole)
    return pl.pallas_call(
        quarters_kernel,
        name="quarters",
        out_shape=[jax.ShapeDtypeStruct(piece, jnp.float32)] + [jax.ShapeDtypeStruct(piece, jnp.bfloat16)] * 3,
        grid=(1,),
        in_specs=[pl.BlockSpec(memory_space=pltpu.SMEM)]
        + [pl.BlockSpec(a.shape, whole) for a in (own, from_x, from_y)],
        out_specs=[out] * 4,
        cost_estimate=pl.CostEstimate(flops=4 * rows * cols, bytes_accessed=2**21, transcendentals=0),
    )(z, own, from_x, from_y)


def added_kernel(*refs):
    out_ref = refs[-1]
    start = 0
    for part in range(0, len(refs) - 1, 4):
        total = refs[part][...]
        for ref in refs[part + 1 : part + 4]:
            total = total + ref[...].astype(jnp.float32)
        out_ref[start : start + total.shape[0], :] = total.astype(out_ref.dtype)
        start += total.shape[0]


def added(parts):
    pieces = [piece for part in parts for piece in part]
    rows, cols = sum(part[0].shape[0] for part in parts), pieces[0].shape[1]
    return pl.pallas_call(
        added_kernel,
        name="added",
        out_shape=jax.ShapeDtypeStruct((rows, cols), jnp.bfloat16),
        cost_estimate=pl.CostEstimate(flops=4 * rows * cols, bytes_accessed=2**20, transcendentals=0),
    )(*pieces)


def joined_kernel(z_ref, *refs, split):
    z = z_ref[0]
    *pieces, out_ref, scr = refs
    rest = pieces[0].shape[0] - split
    for k, piece in enumerate(pieces):
        place = z ^ k
        scr[pl.ds(pl.multiple_of(place * split, split), split), :] = piece[:split, :]
        scr[pl.ds(pl.multiple_of(4 * split + place * rest, rest), rest), :] = piece[split:, :]
    out_ref[...] = scr[...].T


def joined(z, pieces, split):
    rows, cols = pieces[0].shape
    whole = lambda i: (0, 0)
    return pl.pallas_call(
        functools.partial(joined_kernel, split=split),
        name="joined",
        out_shape=jax.ShapeDtypeStruct((cols, 4 * rows), jnp.bfloat16),
        grid=(1,),
        in_specs=[pl.BlockSpec(memory_space=pltpu.SMEM)] + [pl.BlockSpec((rows, cols), whole)] * 4,
        out_specs=pl.BlockSpec((cols, 4 * rows), whole),
        scratch_shapes=[pltpu.VMEM((4 * rows, cols), jnp.bfloat16)],
        cost_estimate=pl.CostEstimate(flops=rows * cols, bytes_accessed=2**21, transcendentals=0),
    )(z, *pieces)


def flipped(array, bits, axis="ctx"):
    return lax.ppermute(array, axis, [(i, i ^ bits) for i in range(lax.axis_size(axis))])


def together(*arrays):
    return lax.optimization_barrier(arrays)


def per_device(inputs, qkv_weight, queries, keys_values, out_grad, lengths):
    f32, bf16 = jnp.float32, jnp.bfloat16
    size = lax.axis_size("ctx")
    planes = lax.axis_size("dp")
    index = lax.axis_index("ctx")
    rows = queries.shape[1]
    assert MOST == 3 * rows
    own = keys_values[0]
    by_two = [(i, i + 2) for i in range(size - 2)]
    mixed = [(i, i + 1) for i in range(0, size, 2)] + [(i, i + 3) for i in range(1, size - 3, 2)]
    back = lambda pairs: [(b, a) for a, b in pairs]
    small = size == 8 and planes == 4
    block = qkv_weight.shape[0]
    x_local = inputs[0]

    d2 = lax.ppermute(own, "ctx", by_two)
    x = lax.ppermute(own, "ctx", mixed)
    w_swapped = flipped(qkv_weight, 1)
    places = jnp.stack([index // 2, index % 2, *map(jnp.int32, (3, 1, 2, 0))])
    d2, x, w_swapped, places = together(d2, x, w_swapped, places)
    r = flipped(d2, 1)
    if small:
        w_own, x_in, r = lax.optimization_barrier((qkv_weight, x_local, r))
        w_x, w_y = flipped(w_own, 2), flipped(w_own, 4)
        x_other = flipped(x_in, 1)
    else:
        w_full = lax.all_gather(qkv_weight, "ctx", axis=0, tiled=True)

    grads = attention(index.reshape(1), lengths, queries[0], out_grad[0], own, d2, r, x)
    if small:
        *grads, w_x, w_y, x_other = lax.optimization_barrier((*grads, w_x, w_y, x_other))
    gq, gqt, kv_own, kv_d2, kv_r, kv_x = grads
    kv_d2 = (kv_d2 + flipped(kv_r, 1)).astype(bf16)
    from_x = lax.ppermute(kv_x, "ctx", back(mixed))

    if small:
        z = lax.axis_index("dp").reshape(1)

        def crossed(pieces):
            return [flipped(piece, k + 1, "dp") for k, piece in enumerate(pieces)]

        gqt_other, kv_d2 = together(flipped(gqt, 1), kv_d2)
        from_two = lax.ppermute(kv_d2, "ctx", back(by_two))
        q_parts = weight_partials(places, gqt, gqt_other, x_local, x_other, block)
        from_two, from_x, w_x, w_y, *q_parts = together(from_two, from_x, w_x, w_y, *q_parts)
        q_own, q_keep, q_x, q_y = q_parts
        q_x, q_y = flipped(q_x, 2), flipped(q_y, 4)
        gkv, gkvt = finish_kv(kv_own, from_two, from_x)
        kv_parts = weight_partials(places, gkvt, flipped(gkvt, 1), x_local, x_other, block)
        w_blocks = (w_own, w_swapped, w_x, flipped(w_x, 1), w_y, flipped(w_y, 1))
        q_x, q_y, *rest = together(q_x, q_y, *kv_parts, *w_blocks)
        (kv_own, kv_keep, kv_x, kv_y), w_blocks = rest[:4], rest[4:]
        q_own, q_x, q_y = middle(q_own, q_keep, q_x, q_y)
        q_x, q_y = flipped(q_x, 2), flipped(q_y, 4)
        kv_x, kv_y = flipped(kv_x, 2), flipped(kv_y, 4)
        q_own, *q_pieces = quarters_of(z, q_own, q_x, q_y)
        q_pieces = crossed(q_pieces)
        kv_own, q_own = together(kv_own, q_own)
        kv_own, kv_x, kv_y = middle(kv_own, kv_keep, kv_x, kv_y)
        kv_x, kv_y = flipped(kv_x, 2), flipped(kv_y, 4)
        kv_x, kv_y, *q_pieces = together(kv_x, kv_y, *q_pieces)
        kv_own, *kv_pieces = quarters_of(z, kv_own, kv_x, kv_y)
        kv_own, w_x, w_y, *kv_pieces = together(kv_own, w_x, w_y, *kv_pieces)
        kv_pieces = crossed(kv_pieces)
        half = block // 2
        w_top, w_bottom = flipped(w_x[:half], 4), flipped(w_y[half:], 2)
        grad_in = input_grad(places, gq, gkv, w_blocks, 0)
        *kv_pieces, grad_in, w_top, w_bottom = together(*kv_pieces, grad_in, w_top, w_bottom)
        w_d = jnp.concatenate([w_top, w_bottom])
        mine = added([(q_own, *q_pieces), (kv_own, *kv_pieces)])
        pieces = crossed([mine] * 3)
        grad_in = input_grad(places, gq, gkv, (w_d, flipped(w_d, 1)), 6, grad_in)
        *pieces, grad_in = together(*pieces, grad_in)
        weight_sum = joined(z, (mine, *pieces), q_own.shape[0])
    else:
        from_two = lax.ppermute(kv_d2, "ctx", back(by_two))
        gkv, _ = finish_kv(kv_own, from_two, from_x)
        grad_qkv = jnp.concatenate([gq, gkv], axis=1)
        grad_in = nt_dot(grad_qkv, w_full).astype(bf16)
        partial = lax.dot_general(
            x_local, grad_qkv, (((0,), (0,)), ((), ())), preferred_element_type=f32
        )
        shard = lax.psum_scatter(partial, "ctx", scatter_dimension=0, tiled=True)
        weight_sum = lax.psum(shard, "dp").astype(bf16)
    return (gq[None], gkv[None], grad_in[None], weight_sum)


def solution(mesh):
    placed = (
        P("dp", "ctx", None),
        P("ctx", None),
        P("dp", "ctx", None),
        P("dp", "ctx", None),
        P("dp", "ctx", None),
        P("dp", None),
    )
    return jax.shard_map(
        per_device,
        mesh=mesh,
        in_specs=placed,
        out_specs=(
            P("dp", "ctx", None),
            P("dp", "ctx", None),
            P("dp", "ctx", None),
            P("ctx", None),
        ),
        check_vma=False,
    )
```

```python
import functools

import jax
import jax.numpy as jnp
from jax import lax
from jax.experimental import pallas as pl
from jax.experimental.pallas import tpu as pltpu
from jax.sharding import PartitionSpec as P

MOST = 1536
NEG_FILL = -1e30
LOG2E = 1.4426950408889634
KEY_STEP = 512
Q_STEP = 256


SMALL_VMEM = 4 * 2**20
VMEM = pl.BlockSpec(memory_space=pltpu.VMEM)


def nt_dot(a, b):
    return lax.dot_general(a, b, (((1,), (1,)), ((), ())), preferred_element_type=jnp.float32)


def nn_dot(a, b):
    return lax.dot_general(a, b, (((1,), (0,)), ((), ())), preferred_element_type=jnp.float32)


def attention_kernel(
    idx_ref, len_ref, q_ref, g_ref, own_ref, d2_ref, r_ref, x_ref,
    gq_ref, gqt_ref, own_out, d2_out, r_out, x_out,
    kv_scr, kt_scr, s_scr, dp_scr, acc_scr,
):
    rows = q_ref.shape[0]
    hd = kv_scr.shape[1] // 2
    heads = q_ref.shape[1] // hd
    wide = heads * Q_STEP
    scaling = hd ** (-0.5)
    index = idx_ref[0]
    parity = lax.rem(index, 2)
    base = (index - 3) * rows
    r_off = pl.multiple_of((1 - parity) * 2 * rows, rows)
    x_off = pl.multiple_of(parity * 2 * rows, rows)
    kv_scr[pl.ds(r_off, rows), :] = r_ref[...]
    kv_scr[pl.ds(x_off, rows), :] = x_ref[...]
    kv_scr[rows : 2 * rows, :] = d2_ref[...]
    kv_scr[3 * rows :, :] = own_ref[...]
    for slot in range(4):
        part = slice(slot * rows, (slot + 1) * rows)
        kt_scr[:, part] = kv_scr[part, :hd].T
    acc_scr[...] = jnp.zeros_like(acc_scr)
    ends = []
    total = -base
    for j in range(len_ref.shape[1]):
        ends.append(total)
        total = total + len_ref[0, j]

    for tile in range(rows // Q_STEP):
        q_rows = slice(tile * Q_STEP, (tile + 1) * Q_STEP)
        first = 3 * rows + tile * Q_STEP
        q_pos = first + (lax.broadcasted_iota(jnp.int32, (1, wide), 1) & (Q_STEP - 1))
        doc_start = jnp.full((1, wide), ends[0], jnp.int32)
        least = ends[0]
        for end in ends[1:]:
            doc_start = jnp.where(q_pos >= end, end, doc_start)
            least = jnp.where(first >= end, end, least)
        q_cat = jnp.concatenate([q_ref[q_rows, h * hd : (h + 1) * hd] for h in range(heads)], axis=0)
        g_cat = jnp.concatenate([g_ref[q_rows, h * hd : (h + 1) * hd] for h in range(heads)], axis=0)
        begin = jnp.maximum(least, 0) // KEY_STEP
        stop = -(-(first + Q_STEP) // KEY_STEP)

        def scores_step(c, carried):
            top, norm, dot = carried
            at = pl.ds(pl.multiple_of(c * KEY_STEP, KEY_STEP), KEY_STEP)
            s = nt_dot(kv_scr[at, :hd], q_cat) * (scaling * LOG2E)
            k_pos = c * KEY_STEP + lax.broadcasted_iota(jnp.int32, (KEY_STEP, wide), 0)
            s = jnp.where((k_pos >= doc_start) & (k_pos <= q_pos), s, NEG_FILL)
            s_scr[at, :] = s
            dp = nt_dot(kv_scr[at, hd:], g_cat)
            dp_scr[at, :] = dp
            s = s.reshape(KEY_STEP // 8, 8, wide)
            above = jnp.maximum(top, jnp.max(s, axis=0))
            shrink = jnp.exp2(top - above)
            e = jnp.exp2(s - above[None])
            norm = norm * shrink + jnp.sum(e, axis=0)
            dot = dot * shrink + jnp.sum(e * dp.reshape(KEY_STEP // 8, 8, wide), axis=0)
            return above, norm, dot

        zero = jnp.zeros((8, wide), jnp.float32)
        tops, norms, dots = lax.fori_loop(
            begin, stop, scores_step, (jnp.full((8, wide), NEG_FILL, jnp.float32), zero, zero)
        )
        top = jnp.max(tops, axis=0, keepdims=True)
        shrink = jnp.exp2(tops - top)
        norm = jnp.sum(norms * shrink, axis=0, keepdims=True)
        delta = jnp.sum(dots * shrink, axis=0, keepdims=True) / norm
        lse = top + jnp.log2(norm)

        def grads_step(c, dq):
            at = pl.ds(pl.multiple_of(c * KEY_STEP, KEY_STEP), KEY_STEP)
            p = jnp.exp2(s_scr[at, :] - lse)
            ds_low = (p * (dp_scr[at, :] - delta)).astype(jnp.bfloat16)
            p_low = p.astype(jnp.bfloat16)
            acc_scr[at, :hd] += nn_dot(ds_low, q_cat)
            acc_scr[at, hd:] += nn_dot(p_low, g_cat)
            return dq + nn_dot(kt_scr[:, at], ds_low)

        dq = lax.fori_loop(begin, stop, grads_step, jnp.zeros((hd, wide), jnp.float32)) * scaling
        for h in range(heads):
            piece = dq[:, h * Q_STEP : (h + 1) * Q_STEP]
            gqt_ref[h * hd : (h + 1) * hd, q_rows] = piece.astype(jnp.bfloat16)
            gq_ref[q_rows, h * hd : (h + 1) * hd] = piece.T.astype(jnp.bfloat16)

    def put(out, at):
        out[:, :hd] = (acc_scr[at, :hd] * scaling).astype(out.dtype)
        out[:, hd:] = acc_scr[at, hd:].astype(out.dtype)

    put(r_out, pl.ds(r_off, rows))
    put(x_out, pl.ds(x_off, rows))
    put(d2_out, slice(rows, 2 * rows))
    put(own_out, slice(3 * rows, 4 * rows))


def attention(index, lengths, q, g, own, d2, r, x):
    rows, width = q.shape
    both = own.shape[1]
    hd = both // 2
    wide = width // hd * Q_STEP
    whole = lambda shape: pl.BlockSpec(shape, lambda i: (0, 0))
    smem = pl.BlockSpec(memory_space=pltpu.SMEM)
    return pl.pallas_call(
        attention_kernel,
        name="attention",
        out_shape=(
            jax.ShapeDtypeStruct((rows, width), jnp.bfloat16),
            jax.ShapeDtypeStruct((width, rows), jnp.bfloat16),
            jax.ShapeDtypeStruct((rows, both), jnp.float32),
            jax.ShapeDtypeStruct((rows, both), jnp.float32),
            jax.ShapeDtypeStruct((rows, both), jnp.float32),
            jax.ShapeDtypeStruct((rows, both), jnp.bfloat16),
        ),
        grid=(1,),
        in_specs=[smem, smem] + [whole((rows, width))] * 2 + [whole((rows, both))] + [VMEM] * 3,
        out_specs=[VMEM] * 6,
        scratch_shapes=[
            pltpu.VMEM((4 * rows, both), jnp.bfloat16),
            pltpu.VMEM((hd, 4 * rows), jnp.bfloat16),
            pltpu.VMEM((4 * rows, wide), jnp.float32),
            pltpu.VMEM((4 * rows, wide), jnp.float32),
            pltpu.VMEM((4 * rows, both), jnp.float32),
        ],
        compiler_params=pltpu.CompilerParams(vmem_limit_bytes=30 * 2**20),
        cost_estimate=pl.CostEstimate(flops=12 * 10**9, bytes_accessed=6 * 2**20, transcendentals=4 * 2**20),
    )(index, lengths, q, g, own, d2, r, x)


def weight_kernel(places, gt_ref, gt_other, x_ref, x_other, own_out, keep_out, to_x, to_y):
    k = pl.program_id(0)
    half = gt_ref.shape[0] // 2
    upper, lower = slice(0, half), slice(half, 2 * half)
    total = nn_dot(gt_ref[...], x_ref[...]) + nn_dot(gt_other[...], x_other[...])
    low = total.astype(jnp.bfloat16)

    @pl.when(k == 3)
    def _():
        own_out[...] = total

    @pl.when(k == 1)
    def _():
        to_x[upper, :] = low[upper, :]
        keep_out[lower, :] = low[lower, :]

    @pl.when(k == 2)
    def _():
        keep_out[upper, :] = low[upper, :]
        to_y[upper, :] = low[lower, :]

    @pl.when(k == 0)
    def _():
        to_x[lower, :] = low[upper, :]
        to_y[lower, :] = low[lower, :]


def weight_partials(places, gt, gt_other, x, x_other, block):
    cols, rows = gt.shape
    chips = x_other.shape[1] // block // 2
    strip = pl.BlockSpec((rows, block), lambda k, s: (0, (s[0] ^ s[2 + k]) * 2 + s[1]))
    return pl.pallas_call(
        weight_kernel,
        name="weight_partials",
        out_shape=[jax.ShapeDtypeStruct((cols, block), jnp.float32)]
        + [jax.ShapeDtypeStruct((cols, block), jnp.bfloat16)] * 3,
        grid_spec=pltpu.PrefetchScalarGridSpec(
            num_scalar_prefetch=1,
            grid=(chips,),
            in_specs=[VMEM] * 2 + [strip] * 2,
            out_specs=[VMEM] * 4,
        ),
        compiler_params=pltpu.CompilerParams(vmem_limit_bytes=12 * 2**20),
        cost_estimate=pl.CostEstimate(
            flops=4 * cols * rows * block * chips, bytes_accessed=8 * 2**20, transcendentals=0
        ),
    )(places, gt, gt_other, x, x_other)


def row_loop(rows, step, body):
    def turn(i, carried):
        body(pl.multiple_of(i * step, step))
        return carried

    lax.fori_loop(0, rows // step, turn, 0)


def middle_kernel(own_ref, keep_ref, from_x, from_y, own_out, next_x, next_y):
    f32 = jnp.float32
    half = own_ref.shape[0] // 2
    step = 32

    def body(at):
        top, low = pl.ds(at, step), pl.ds(half + at, step)
        own_out[top, :] = own_ref[top, :] + from_x[top, :].astype(f32)
        own_out[low, :] = own_ref[low, :] + from_y[top, :].astype(f32)
        next_y[top, :] = (keep_ref[top, :].astype(f32) + from_x[low, :].astype(f32)).astype(next_y.dtype)
        next_x[top, :] = (keep_ref[low, :].astype(f32) + from_y[low, :].astype(f32)).astype(next_x.dtype)

    row_loop(half, step, body)


def middle(own, keep, from_x, from_y):
    rows, cols = own.shape
    half = jax.ShapeDtypeStruct((rows // 2, cols), jnp.bfloat16)
    return pl.pallas_call(
        middle_kernel,
        name="middle",
        out_shape=[jax.ShapeDtypeStruct(own.shape, jnp.float32), half, half],
        in_specs=[VMEM] * 4,
        out_specs=[VMEM] * 3,
        compiler_params=pltpu.CompilerParams(vmem_limit_bytes=SMALL_VMEM),
        cost_estimate=pl.CostEstimate(flops=4 * rows * cols, bytes_accessed=2**21, transcendentals=0),
    )(own, keep, from_x, from_y)


def input_kernel(places, gq_ref, gkv_ref, *refs, count):
    out_ref = refs[-1]
    k = pl.program_id(0)
    q_cols = gq_ref.shape[1]
    for turn, w_ref in enumerate(refs[:count]):
        @pl.when(k == turn)
        def _(w_ref=w_ref):
            out_ref[...] = (
                nt_dot(gq_ref[...], w_ref[:, :q_cols]) + nt_dot(gkv_ref[...], w_ref[:, q_cols:])
            ).astype(out_ref.dtype)


def input_grad(places, gq, gkv, blocks, start, earlier=None):
    rows = gq.shape[0]
    block, cols = blocks[0].shape
    count = len(blocks)
    total = lax.axis_size("ctx") * block
    whole = lambda k, s: (0, 0)
    before = [] if earlier is None else [earlier]
    return pl.pallas_call(
        functools.partial(input_kernel, count=count),
        name="input_grad",
        out_shape=jax.ShapeDtypeStruct((rows, total), jnp.bfloat16),
        grid_spec=pltpu.PrefetchScalarGridSpec(
            num_scalar_prefetch=1,
            grid=(count,),
            in_specs=[pl.BlockSpec(gq.shape, whole), pl.BlockSpec(gkv.shape, whole)]
            + [pl.BlockSpec((block, cols), whole)] * count
            + [pl.BlockSpec(memory_space=pl.ANY)] * len(before),
            out_specs=pl.BlockSpec((rows, block), lambda k, s: (0, (s[0] * 2 + s[1]) ^ (start + k))),
        ),
        input_output_aliases={3 + count: 0} if before else {},
        compiler_params=pltpu.CompilerParams(vmem_limit_bytes=20 * 2**20),
        cost_estimate=pl.CostEstimate(
            flops=2 * rows * cols * block * count, bytes_accessed=11 * 2**20, transcendentals=0
        ),
    )(places, gq, gkv, *blocks, *before)


def finish_kernel(own_ref, two_ref, x_ref, out_ref, out_t_ref):
    step = 128

    def body(start):
        at = pl.ds(start, step)
        total = own_ref[at, :] + two_ref[at, :].astype(jnp.float32) + x_ref[at, :].astype(jnp.float32)
        out_ref[at, :] = total.astype(out_ref.dtype)
        out_t_ref[:, at] = total.T.astype(out_t_ref.dtype)

    row_loop(own_ref.shape[0], step, body)


def finish_kv(own, from_two, from_x):
    rows, cols = own.shape
    return pl.pallas_call(
        finish_kernel,
        name="finish_kv",
        out_shape=(
            jax.ShapeDtypeStruct((rows, cols), jnp.bfloat16),
            jax.ShapeDtypeStruct((cols, rows), jnp.bfloat16),
        ),
        in_specs=[VMEM] * 3,
        out_specs=[VMEM] * 2,
        compiler_params=pltpu.CompilerParams(vmem_limit_bytes=SMALL_VMEM),
        cost_estimate=pl.CostEstimate(flops=4 * rows * cols, bytes_accessed=2**21, transcendentals=0),
    )(own, from_two, from_x)


def quarters_kernel(z_ref, own_ref, x_ref, y_ref, mine_out, *outs):
    z = z_ref[0]
    quarter = mine_out.shape[0]
    step = 32
    for k, out in enumerate((mine_out, *outs)):
        place = z ^ k

        def body(start, place=place, out=out):
            at = pl.ds(pl.multiple_of(place * quarter + start, step), step)
            half = pl.ds(pl.multiple_of(lax.rem(place, 2) * quarter + start, step), step)
            add = jnp.where(place < 2, y_ref[half, :].astype(jnp.float32), x_ref[half, :].astype(jnp.float32))
            out[pl.ds(start, step), :] = (own_ref[at, :] + add).astype(out.dtype)

        row_loop(quarter, step, body)


def quarters_of(z, own, from_x, from_y):
    rows, cols = own.shape
    piece = (rows // 4, cols)
    return pl.pallas_call(
        quarters_kernel,
        name="quarters",
        out_shape=[jax.ShapeDtypeStruct(piece, jnp.float32)] + [jax.ShapeDtypeStruct(piece, jnp.bfloat16)] * 3,
        in_specs=[pl.BlockSpec(memory_space=pltpu.SMEM)] + [VMEM] * 3,
        out_specs=[VMEM] * 4,
        compiler_params=pltpu.CompilerParams(vmem_limit_bytes=SMALL_VMEM),
        cost_estimate=pl.CostEstimate(flops=4 * rows * cols, bytes_accessed=2**21, transcendentals=0),
    )(z, own, from_x, from_y)


def added_kernel(*refs):
    out_ref = refs[-1]
    first = 0
    step = 32
    for part in range(0, len(refs) - 1, 4):
        own = refs[part]

        def body(start, part=part, first=first):
            at = pl.ds(start, step)
            total = refs[part][at, :]
            for ref in refs[part + 1 : part + 4]:
                total = total + ref[at, :].astype(jnp.float32)
            out_ref[pl.ds(pl.multiple_of(first + start, step), step), :] = total.astype(out_ref.dtype)

        row_loop(own.shape[0], step, body)
        first += own.shape[0]


def added(parts):
    pieces = [piece for part in parts for piece in part]
    rows, cols = sum(part[0].shape[0] for part in parts), pieces[0].shape[1]
    return pl.pallas_call(
        added_kernel,
        name="added",
        out_shape=jax.ShapeDtypeStruct((rows, cols), jnp.bfloat16),
        in_specs=[VMEM] * len(pieces),
        out_specs=VMEM,
        compiler_params=pltpu.CompilerParams(vmem_limit_bytes=SMALL_VMEM),
        cost_estimate=pl.CostEstimate(flops=4 * rows * cols, bytes_accessed=2**20, transcendentals=0),
    )(*pieces)


def joined_kernel(z_ref, *refs, split):
    z = z_ref[0]
    *pieces, out_ref, scr = refs
    rest = pieces[0].shape[0] - split
    for k, piece in enumerate(pieces):
        place = z ^ k
        scr[pl.ds(pl.multiple_of(place * split, split), split), :] = piece[:split, :]
        scr[pl.ds(pl.multiple_of(4 * split + place * rest, rest), rest), :] = piece[split:, :]

    def body(start):
        at = pl.ds(start, 128)
        out_ref[:, at] = scr[at, :].T

    row_loop(scr.shape[0], 128, body)


def joined(z, pieces, split):
    rows, cols = pieces[0].shape
    return pl.pallas_call(
        functools.partial(joined_kernel, split=split),
        name="joined",
        out_shape=jax.ShapeDtypeStruct((cols, 4 * rows), jnp.bfloat16),
        in_specs=[pl.BlockSpec(memory_space=pltpu.SMEM)] + [VMEM] * 4,
        out_specs=VMEM,
        scratch_shapes=[pltpu.VMEM((4 * rows, cols), jnp.bfloat16)],
        compiler_params=pltpu.CompilerParams(vmem_limit_bytes=SMALL_VMEM),
        cost_estimate=pl.CostEstimate(flops=rows * cols, bytes_accessed=2**21, transcendentals=0),
    )(z, *pieces)


def flipped(array, bits, axis="ctx"):
    return lax.ppermute(array, axis, [(i, i ^ bits) for i in range(lax.axis_size(axis))])


def together(*arrays):
    return lax.optimization_barrier(arrays)


def per_device(inputs, qkv_weight, queries, keys_values, out_grad, lengths):
    f32, bf16 = jnp.float32, jnp.bfloat16
    size = lax.axis_size("ctx")
    planes = lax.axis_size("dp")
    index = lax.axis_index("ctx")
    rows = queries.shape[1]
    assert MOST == 3 * rows
    own = keys_values[0]
    by_two = [(i, i + 2) for i in range(size - 2)]
    mixed = [(i, i + 1) for i in range(0, size, 2)] + [(i, i + 3) for i in range(1, size - 3, 2)]
    back = lambda pairs: [(b, a) for a, b in pairs]
    small = size == 8 and planes == 4
    block = qkv_weight.shape[0]
    x_local = inputs[0]

    d2 = lax.ppermute(own, "ctx", by_two)
    x = lax.ppermute(own, "ctx", mixed)
    w_swapped = flipped(qkv_weight, 1)
    places = jnp.stack([index // 2, index % 2, *map(jnp.int32, (3, 1, 2, 0))])
    d2, x, w_swapped, places = together(d2, x, w_swapped, places)
    r = flipped(d2, 1)
    if small:
        w_own, x_in, r = lax.optimization_barrier((qkv_weight, x_local, r))
        w_x, w_y = flipped(w_own, 2), flipped(w_own, 4)
        x_other = flipped(x_in, 1)
    else:
        w_full = lax.all_gather(qkv_weight, "ctx", axis=0, tiled=True)

    grads = attention(index.reshape(1), lengths, queries[0], out_grad[0], own, d2, r, x)
    if small:
        *grads, w_x, w_y, x_other = lax.optimization_barrier((*grads, w_x, w_y, x_other))
    gq, gqt, kv_own, kv_d2, kv_r, kv_x = grads
    kv_d2 = (kv_d2 + flipped(kv_r, 1)).astype(bf16)
    from_x = lax.ppermute(kv_x, "ctx", back(mixed))

    if small:
        z = lax.axis_index("dp").reshape(1)

        def crossed(pieces):
            return [flipped(piece, k + 1, "dp") for k, piece in enumerate(pieces)]

        gqt_other, kv_d2 = together(flipped(gqt, 1), kv_d2)
        from_two = lax.ppermute(kv_d2, "ctx", back(by_two))
        q_parts = weight_partials(places, gqt, gqt_other, x_local, x_other, block)
        from_two, from_x, w_x, w_y, *q_parts = together(from_two, from_x, w_x, w_y, *q_parts)
        q_own, q_keep, q_x, q_y = q_parts
        q_x, q_y = flipped(q_x, 2), flipped(q_y, 4)
        gkv, gkvt = finish_kv(kv_own, from_two, from_x)
        kv_parts = weight_partials(places, gkvt, flipped(gkvt, 1), x_local, x_other, block)
        w_blocks = (w_own, w_swapped, w_x, flipped(w_x, 1), w_y, flipped(w_y, 1))
        q_x, q_y, *rest = together(q_x, q_y, *kv_parts, *w_blocks)
        (kv_own, kv_keep, kv_x, kv_y), w_blocks = rest[:4], rest[4:]
        q_own, q_x, q_y = middle(q_own, q_keep, q_x, q_y)
        q_x, q_y = flipped(q_x, 2), flipped(q_y, 4)
        kv_x, kv_y = flipped(kv_x, 2), flipped(kv_y, 4)
        q_own, *q_pieces = quarters_of(z, q_own, q_x, q_y)
        q_pieces = crossed(q_pieces)
        kv_own, q_own = together(kv_own, q_own)
        kv_own, kv_x, kv_y = middle(kv_own, kv_keep, kv_x, kv_y)
        kv_x, kv_y = flipped(kv_x, 2), flipped(kv_y, 4)
        kv_x, kv_y, *q_pieces = together(kv_x, kv_y, *q_pieces)
        kv_own, *kv_pieces = quarters_of(z, kv_own, kv_x, kv_y)
        kv_own, w_x, w_y, *kv_pieces = together(kv_own, w_x, w_y, *kv_pieces)
        kv_pieces = crossed(kv_pieces)
        half = block // 2
        w_top, w_bottom = flipped(w_x[:half], 4), flipped(w_y[half:], 2)
        grad_in = input_grad(places, gq, gkv, w_blocks, 0)
        *kv_pieces, grad_in, w_top, w_bottom = together(*kv_pieces, grad_in, w_top, w_bottom)
        w_d = jnp.concatenate([w_top, w_bottom])
        mine = added([(q_own, *q_pieces), (kv_own, *kv_pieces)])
        pieces = crossed([mine] * 3)
        grad_in = input_grad(places, gq, gkv, (w_d, flipped(w_d, 1)), 6, grad_in)
        *pieces, grad_in = together(*pieces, grad_in)
        weight_sum = joined(z, (mine, *pieces), q_own.shape[0])
    else:
        from_two = lax.ppermute(kv_d2, "ctx", back(by_two))
        gkv, _ = finish_kv(kv_own, from_two, from_x)
        grad_qkv = jnp.concatenate([gq, gkv], axis=1)
        grad_in = nt_dot(grad_qkv, w_full).astype(bf16)
        partial = lax.dot_general(
            x_local, grad_qkv, (((0,), (0,)), ((), ())), preferred_element_type=f32
        )
        shard = lax.psum_scatter(partial, "ctx", scatter_dimension=0, tiled=True)
        weight_sum = lax.psum(shard, "dp").astype(bf16)
    return (gq[None], gkv[None], grad_in[None], weight_sum)


def solution(mesh):
    placed = (
        P("dp", "ctx", None),
        P("ctx", None),
        P("dp", "ctx", None),
        P("dp", "ctx", None),
        P("dp", "ctx", None),
        P("dp", None),
    )
    return jax.shard_map(
        per_device,
        mesh=mesh,
        in_specs=placed,
        out_specs=(
            P("dp", "ctx", None),
            P("dp", "ctx", None),
            P("dp", "ctx", None),
            P("ctx", None),
        ),
        check_vma=False,
    )
```

```python
import functools

import jax
import jax.numpy as jnp
from jax import lax
from jax.experimental import pallas as pl
from jax.experimental.pallas import tpu as pltpu
from jax.sharding import PartitionSpec as P

MOST = 1536
NEG_FILL = -1e30
LOG2E = 1.4426950408889634
KEY_STEP = 512
Q_STEP = 256


SMALL_VMEM = 4 * 2**20
VMEM = pl.BlockSpec(memory_space=pltpu.VMEM)


def nt_dot(a, b):
    return lax.dot_general(a, b, (((1,), (1,)), ((), ())), preferred_element_type=jnp.float32)


def nn_dot(a, b):
    return lax.dot_general(a, b, (((1,), (0,)), ((), ())), preferred_element_type=jnp.float32)


def attention_kernel(
    info_ref, q_ref, g_ref, own_ref, d2_ref, r_ref, x_ref,
    gq_ref, gqt_ref, own_out, d2_out, r_out, x_out,
    kv_scr, kt_scr, s_scr, dp_scr, acc_scr,
):
    rows = q_ref.shape[0]
    hd = kv_scr.shape[1] // 2
    heads = q_ref.shape[1] // hd
    wide = heads * Q_STEP
    scaling = hd ** (-0.5)
    index = info_ref[0]
    parity = lax.rem(index, 2)
    base = (index - 3) * rows
    r_off = pl.multiple_of((1 - parity) * 2 * rows, rows)
    x_off = pl.multiple_of(parity * 2 * rows, rows)
    kv_scr[pl.ds(r_off, rows), :] = r_ref[...]
    kv_scr[pl.ds(x_off, rows), :] = x_ref[...]
    kv_scr[rows : 2 * rows, :] = d2_ref[...]
    kv_scr[3 * rows :, :] = own_ref[...]
    for slot in range(4):
        part = slice(slot * rows, (slot + 1) * rows)
        kt_scr[:, part] = kv_scr[part, :hd].T
    acc_scr[...] = jnp.zeros_like(acc_scr)
    ends = []
    total = -base
    for j in range(1, info_ref.shape[0]):
        ends.append(total)
        total = total + info_ref[j]

    for tile in range(rows // Q_STEP):
        q_rows = slice(tile * Q_STEP, (tile + 1) * Q_STEP)
        first = 3 * rows + tile * Q_STEP
        q_pos = first + (lax.broadcasted_iota(jnp.int32, (1, wide), 1) & (Q_STEP - 1))
        doc_start = jnp.full((1, wide), ends[0], jnp.int32)
        least = ends[0]
        for end in ends[1:]:
            doc_start = jnp.where(q_pos >= end, end, doc_start)
            least = jnp.where(first >= end, end, least)
        q_cat = jnp.concatenate([q_ref[q_rows, h * hd : (h + 1) * hd] for h in range(heads)], axis=0)
        g_cat = jnp.concatenate([g_ref[q_rows, h * hd : (h + 1) * hd] for h in range(heads)], axis=0)
        begin = jnp.maximum(least, 0) // KEY_STEP
        stop = -(-(first + Q_STEP) // KEY_STEP)

        def scores_step(c, carried):
            top, norm, dot = carried
            at = pl.ds(pl.multiple_of(c * KEY_STEP, KEY_STEP), KEY_STEP)
            s = nt_dot(kv_scr[at, :hd], q_cat) * (scaling * LOG2E)
            k_pos = c * KEY_STEP + lax.broadcasted_iota(jnp.int32, (KEY_STEP, wide), 0)
            s = jnp.where((k_pos >= doc_start) & (k_pos <= q_pos), s, NEG_FILL)
            s_scr[at, :] = s
            dp = nt_dot(kv_scr[at, hd:], g_cat)
            dp_scr[at, :] = dp
            s = s.reshape(KEY_STEP // 8, 8, wide)
            above = jnp.maximum(top, jnp.max(s, axis=0))
            shrink = jnp.exp2(top - above)
            e = jnp.exp2(s - above[None])
            norm = norm * shrink + jnp.sum(e, axis=0)
            dot = dot * shrink + jnp.sum(e * dp.reshape(KEY_STEP // 8, 8, wide), axis=0)
            return above, norm, dot

        zero = jnp.zeros((8, wide), jnp.float32)
        tops, norms, dots = lax.fori_loop(
            begin, stop, scores_step, (jnp.full((8, wide), NEG_FILL, jnp.float32), zero, zero)
        )
        top = jnp.max(tops, axis=0, keepdims=True)
        shrink = jnp.exp2(tops - top)
        norm = jnp.sum(norms * shrink, axis=0, keepdims=True)
        delta = jnp.sum(dots * shrink, axis=0, keepdims=True) / norm
        lse = top + jnp.log2(norm)

        def grads_step(c, dq):
            at = pl.ds(pl.multiple_of(c * KEY_STEP, KEY_STEP), KEY_STEP)
            p = jnp.exp2(s_scr[at, :] - lse)
            ds_low = (p * (dp_scr[at, :] - delta)).astype(jnp.bfloat16)
            p_low = p.astype(jnp.bfloat16)
            acc_scr[at, :hd] += nn_dot(ds_low, q_cat)
            acc_scr[at, hd:] += nn_dot(p_low, g_cat)
            return dq + nn_dot(kt_scr[:, at], ds_low)

        dq = lax.fori_loop(begin, stop, grads_step, jnp.zeros((hd, wide), jnp.float32)) * scaling
        for h in range(heads):
            piece = dq[:, h * Q_STEP : (h + 1) * Q_STEP]
            gqt_ref[h * hd : (h + 1) * hd, q_rows] = piece.astype(jnp.bfloat16)
            gq_ref[q_rows, h * hd : (h + 1) * hd] = piece.T.astype(jnp.bfloat16)

    def put(out, at):
        out[:, :hd] = (acc_scr[at, :hd] * scaling).astype(out.dtype)
        out[:, hd:] = acc_scr[at, hd:].astype(out.dtype)

    put(r_out, pl.ds(r_off, rows))
    put(x_out, pl.ds(x_off, rows))
    put(d2_out, slice(rows, 2 * rows))
    put(own_out, slice(3 * rows, 4 * rows))


def attention(info, q, g, own, d2, r, x):
    rows, width = q.shape
    both = own.shape[1]
    hd = both // 2
    wide = width // hd * Q_STEP
    smem = pl.BlockSpec(memory_space=pltpu.SMEM)
    return pl.pallas_call(
        attention_kernel,
        name="attention",
        out_shape=(
            jax.ShapeDtypeStruct((rows, width), jnp.bfloat16),
            jax.ShapeDtypeStruct((width, rows), jnp.bfloat16),
            jax.ShapeDtypeStruct((rows, both), jnp.float32),
            jax.ShapeDtypeStruct((rows, both), jnp.float32),
            jax.ShapeDtypeStruct((rows, both), jnp.float32),
            jax.ShapeDtypeStruct((rows, both), jnp.bfloat16),
        ),
        in_specs=[smem] + [VMEM] * 6,
        out_specs=[VMEM] * 6,
        scratch_shapes=[
            pltpu.VMEM((4 * rows, both), jnp.bfloat16),
            pltpu.VMEM((hd, 4 * rows), jnp.bfloat16),
            pltpu.VMEM((4 * rows, wide), jnp.float32),
            pltpu.VMEM((4 * rows, wide), jnp.float32),
            pltpu.VMEM((4 * rows, both), jnp.float32),
        ],
        compiler_params=pltpu.CompilerParams(vmem_limit_bytes=30 * 2**20),
        cost_estimate=pl.CostEstimate(flops=12 * 10**9, bytes_accessed=6 * 2**20, transcendentals=4 * 2**20),
    )(info, q, g, own, d2, r, x)


def staged_kernel(*refs):
    count = len(refs) // 2
    for source, target in zip(refs[:count], refs[count:]):
        step = 64

        def body(start, source=source, target=target):
            target[pl.ds(start, step), :] = source[pl.ds(start, step), :]

        row_loop(source.shape[0], step, body)


def staged(*arrays):
    return pl.pallas_call(
        staged_kernel,
        name="staged",
        out_shape=[jax.ShapeDtypeStruct(a.shape, a.dtype) for a in arrays],
        in_specs=[VMEM] * len(arrays),
        out_specs=[VMEM] * len(arrays),
        compiler_params=pltpu.CompilerParams(vmem_limit_bytes=SMALL_VMEM),
        cost_estimate=pl.CostEstimate(flops=2**20, bytes_accessed=3 * 2**20, transcendentals=0),
    )(*arrays)


def weight_kernel(places, gt_ref, gt_other, x_ref, x_other, own_out, keep_out, to_x, to_y):
    k = pl.program_id(0)
    half = gt_ref.shape[0] // 2
    upper, lower = slice(0, half), slice(half, 2 * half)
    total = nn_dot(gt_ref[...], x_ref[...]) + nn_dot(gt_other[...], x_other[...])
    low = total.astype(jnp.bfloat16)

    @pl.when(k == 3)
    def _():
        own_out[...] = total

    @pl.when(k == 1)
    def _():
        to_x[upper, :] = low[upper, :]
        keep_out[lower, :] = low[lower, :]

    @pl.when(k == 2)
    def _():
        keep_out[upper, :] = low[upper, :]
        to_y[upper, :] = low[lower, :]

    @pl.when(k == 0)
    def _():
        to_x[lower, :] = low[upper, :]
        to_y[lower, :] = low[lower, :]


def weight_partials(places, gt, gt_other, x, x_other, block):
    cols, rows = gt.shape
    chips = x_other.shape[1] // block // 2
    strip = pl.BlockSpec((rows, block), lambda k, s: (0, (s[0] ^ s[2 + k]) * 2 + s[1]))
    return pl.pallas_call(
        weight_kernel,
        name="weight_partials",
        out_shape=[jax.ShapeDtypeStruct((cols, block), jnp.float32)]
        + [jax.ShapeDtypeStruct((cols, block), jnp.bfloat16)] * 3,
        grid_spec=pltpu.PrefetchScalarGridSpec(
            num_scalar_prefetch=1,
            grid=(chips,),
            in_specs=[VMEM] * 2 + [strip] * 2,
            out_specs=[VMEM] * 4,
        ),
        compiler_params=pltpu.CompilerParams(vmem_limit_bytes=12 * 2**20),
        cost_estimate=pl.CostEstimate(
            flops=4 * cols * rows * block * chips, bytes_accessed=8 * 2**20, transcendentals=0
        ),
    )(places, gt, gt_other, x, x_other)


def row_loop(rows, step, body):
    def turn(i, carried):
        body(pl.multiple_of(i * step, step))
        return carried

    lax.fori_loop(0, rows // step, turn, 0)


def middle_kernel(own_ref, keep_ref, from_x, from_y, own_out, next_x, next_y):
    f32 = jnp.float32
    half = own_ref.shape[0] // 2
    step = 32

    def body(at):
        top, low = pl.ds(at, step), pl.ds(half + at, step)
        own_out[top, :] = own_ref[top, :] + from_x[top, :].astype(f32)
        own_out[low, :] = own_ref[low, :] + from_y[top, :].astype(f32)
        next_y[top, :] = (keep_ref[top, :].astype(f32) + from_x[low, :].astype(f32)).astype(next_y.dtype)
        next_x[top, :] = (keep_ref[low, :].astype(f32) + from_y[low, :].astype(f32)).astype(next_x.dtype)

    row_loop(half, step, body)


def middle(own, keep, from_x, from_y):
    rows, cols = own.shape
    half = jax.ShapeDtypeStruct((rows // 2, cols), jnp.bfloat16)
    return pl.pallas_call(
        middle_kernel,
        name="middle",
        out_shape=[jax.ShapeDtypeStruct(own.shape, jnp.float32), half, half],
        in_specs=[VMEM] * 4,
        out_specs=[VMEM] * 3,
        compiler_params=pltpu.CompilerParams(vmem_limit_bytes=SMALL_VMEM),
        cost_estimate=pl.CostEstimate(flops=4 * rows * cols, bytes_accessed=2**21, transcendentals=0),
    )(own, keep, from_x, from_y)


def input_kernel(places, gq_ref, gkv_ref, *refs, count):
    out_ref = refs[-1]
    k = pl.program_id(0)
    q_cols = gq_ref.shape[1]
    for turn, w_ref in enumerate(refs[:count]):
        @pl.when(k == turn)
        def _(w_ref=w_ref):
            out_ref[...] = (
                nt_dot(gq_ref[...], w_ref[:, :q_cols]) + nt_dot(gkv_ref[...], w_ref[:, q_cols:])
            ).astype(out_ref.dtype)


def input_grad(places, gq, gkv, blocks, start, earlier=None):
    rows = gq.shape[0]
    block, cols = blocks[0].shape
    count = len(blocks)
    total = lax.axis_size("ctx") * block
    whole = lambda k, s: (0, 0)
    before = [] if earlier is None else [earlier]
    return pl.pallas_call(
        functools.partial(input_kernel, count=count),
        name="input_grad",
        out_shape=jax.ShapeDtypeStruct((rows, total), jnp.bfloat16),
        grid_spec=pltpu.PrefetchScalarGridSpec(
            num_scalar_prefetch=1,
            grid=(count,),
            in_specs=[pl.BlockSpec(gq.shape, whole), pl.BlockSpec(gkv.shape, whole)]
            + [pl.BlockSpec((block, cols), whole)] * count
            + [pl.BlockSpec(memory_space=pl.ANY)] * len(before),
            out_specs=pl.BlockSpec((rows, block), lambda k, s: (0, (s[0] * 2 + s[1]) ^ (start + k))),
        ),
        input_output_aliases={3 + count: 0} if before else {},
        compiler_params=pltpu.CompilerParams(vmem_limit_bytes=20 * 2**20),
        cost_estimate=pl.CostEstimate(
            flops=2 * rows * cols * block * count, bytes_accessed=11 * 2**20, transcendentals=0
        ),
    )(places, gq, gkv, *blocks, *before)


def finish_kernel(own_ref, two_ref, x_ref, out_ref, out_t_ref):
    step = 128

    def body(start):
        at = pl.ds(start, step)
        total = own_ref[at, :] + two_ref[at, :].astype(jnp.float32) + x_ref[at, :].astype(jnp.float32)
        out_ref[at, :] = total.astype(out_ref.dtype)
        out_t_ref[:, at] = total.T.astype(out_t_ref.dtype)

    row_loop(own_ref.shape[0], step, body)


def finish_kv(own, from_two, from_x):
    rows, cols = own.shape
    return pl.pallas_call(
        finish_kernel,
        name="finish_kv",
        out_shape=(
            jax.ShapeDtypeStruct((rows, cols), jnp.bfloat16),
            jax.ShapeDtypeStruct((cols, rows), jnp.bfloat16),
        ),
        in_specs=[VMEM] * 3,
        out_specs=[VMEM] * 2,
        compiler_params=pltpu.CompilerParams(vmem_limit_bytes=SMALL_VMEM),
        cost_estimate=pl.CostEstimate(flops=4 * rows * cols, bytes_accessed=2**21, transcendentals=0),
    )(own, from_two, from_x)


def quarters_kernel(z_ref, own_ref, x_ref, y_ref, mine_out, *outs):
    z = z_ref[0]
    quarter = mine_out.shape[0]
    step = 32
    for k, out in enumerate((mine_out, *outs)):
        place = z ^ k

        def body(start, place=place, out=out):
            at = pl.ds(pl.multiple_of(place * quarter + start, step), step)
            half = pl.ds(pl.multiple_of(lax.rem(place, 2) * quarter + start, step), step)
            add = jnp.where(place < 2, y_ref[half, :].astype(jnp.float32), x_ref[half, :].astype(jnp.float32))
            out[pl.ds(start, step), :] = (own_ref[at, :] + add).astype(out.dtype)

        row_loop(quarter, step, body)


def quarters_of(z, own, from_x, from_y):
    rows, cols = own.shape
    piece = (rows // 4, cols)
    return pl.pallas_call(
        quarters_kernel,
        name="quarters",
        out_shape=[jax.ShapeDtypeStruct(piece, jnp.float32)] + [jax.ShapeDtypeStruct(piece, jnp.bfloat16)] * 3,
        in_specs=[pl.BlockSpec(memory_space=pltpu.SMEM)] + [VMEM] * 3,
        out_specs=[VMEM] * 4,
        compiler_params=pltpu.CompilerParams(vmem_limit_bytes=SMALL_VMEM),
        cost_estimate=pl.CostEstimate(flops=4 * rows * cols, bytes_accessed=2**21, transcendentals=0),
    )(z, own, from_x, from_y)


def added_kernel(*refs):
    out_ref = refs[-1]
    first = 0
    step = 32
    for part in range(0, len(refs) - 1, 4):
        own = refs[part]

        def body(start, part=part, first=first):
            at = pl.ds(start, step)
            total = refs[part][at, :]
            for ref in refs[part + 1 : part + 4]:
                total = total + ref[at, :].astype(jnp.float32)
            out_ref[pl.ds(pl.multiple_of(first + start, step), step), :] = total.astype(out_ref.dtype)

        row_loop(own.shape[0], step, body)
        first += own.shape[0]


def added(parts):
    pieces = [piece for part in parts for piece in part]
    rows, cols = sum(part[0].shape[0] for part in parts), pieces[0].shape[1]
    return pl.pallas_call(
        added_kernel,
        name="added",
        out_shape=jax.ShapeDtypeStruct((rows, cols), jnp.bfloat16),
        in_specs=[VMEM] * len(pieces),
        out_specs=VMEM,
        compiler_params=pltpu.CompilerParams(vmem_limit_bytes=SMALL_VMEM),
        cost_estimate=pl.CostEstimate(flops=4 * rows * cols, bytes_accessed=2**20, transcendentals=0),
    )(*pieces)


def joined_kernel(z_ref, *refs, split):
    z = z_ref[0]
    *pieces, out_ref, scr = refs
    rest = pieces[0].shape[0] - split
    for k, piece in enumerate(pieces):
        place = z ^ k
        scr[pl.ds(pl.multiple_of(place * split, split), split), :] = piece[:split, :]
        scr[pl.ds(pl.multiple_of(4 * split + place * rest, rest), rest), :] = piece[split:, :]

    def body(start):
        at = pl.ds(start, 128)
        out_ref[:, at] = scr[at, :].T

    row_loop(scr.shape[0], 128, body)


def joined(z, pieces, split):
    rows, cols = pieces[0].shape
    return pl.pallas_call(
        functools.partial(joined_kernel, split=split),
        name="joined",
        out_shape=jax.ShapeDtypeStruct((cols, 4 * rows), jnp.bfloat16),
        in_specs=[pl.BlockSpec(memory_space=pltpu.SMEM)] + [VMEM] * 4,
        out_specs=VMEM,
        scratch_shapes=[pltpu.VMEM((4 * rows, cols), jnp.bfloat16)],
        compiler_params=pltpu.CompilerParams(vmem_limit_bytes=SMALL_VMEM),
        cost_estimate=pl.CostEstimate(flops=rows * cols, bytes_accessed=2**21, transcendentals=0),
    )(z, *pieces)


def flipped(array, bits, axis="ctx"):
    return lax.ppermute(array, axis, [(i, i ^ bits) for i in range(lax.axis_size(axis))])


def together(*arrays):
    return lax.optimization_barrier(arrays)


def per_device(inputs, qkv_weight, queries, keys_values, out_grad, lengths):
    f32, bf16 = jnp.float32, jnp.bfloat16
    size = lax.axis_size("ctx")
    planes = lax.axis_size("dp")
    index = lax.axis_index("ctx")
    rows = queries.shape[1]
    assert MOST == 3 * rows
    own = keys_values[0]
    by_two = [(i, i + 2) for i in range(size - 2)]
    mixed = [(i, i + 1) for i in range(0, size, 2)] + [(i, i + 3) for i in range(1, size - 3, 2)]
    back = lambda pairs: [(b, a) for a, b in pairs]
    small = size == 8 and planes == 4
    block = qkv_weight.shape[0]
    x_local = inputs[0]

    d2 = lax.ppermute(own, "ctx", by_two)
    x = lax.ppermute(own, "ctx", mixed)
    w_swapped = flipped(qkv_weight, 1)
    places = jnp.stack([index // 2, index % 2, *map(jnp.int32, (3, 1, 2, 0))])
    info = jnp.concatenate([index.reshape(1), lengths[0]])
    q, g, near = staged(queries[0], out_grad[0], own)
    d2, x, w_swapped, places, info, q, g, near = together(d2, x, w_swapped, places, info, q, g, near)
    r = flipped(d2, 1)
    if small:
        w_own, x_in, r = lax.optimization_barrier((qkv_weight, x_local, r))
        w_x, w_y = flipped(w_own, 2), flipped(w_own, 4)
        x_other = flipped(x_in, 1)
    else:
        w_full = lax.all_gather(qkv_weight, "ctx", axis=0, tiled=True)

    grads = attention(info, q, g, near, d2, r, x)
    if small:
        *grads, x_other = together(*grads, x_other)
    gq, gqt, kv_own, kv_d2, kv_r, kv_x = grads
    kv_d2 = (kv_d2 + flipped(kv_r, 1)).astype(bf16)
    from_x = lax.ppermute(kv_x, "ctx", back(mixed))

    if small:
        z = lax.axis_index("dp").reshape(1)

        def crossed(pieces):
            return [flipped(piece, k + 1, "dp") for k, piece in enumerate(pieces)]

        gqt_other, kv_d2, w_x, w_y = together(flipped(gqt, 1), kv_d2, w_x, w_y)
        from_two = lax.ppermute(kv_d2, "ctx", back(by_two))
        q_parts = weight_partials(places, gqt, gqt_other, x_local, x_other, block)
        from_two, from_x, w_x, w_y, *q_parts = together(from_two, from_x, w_x, w_y, *q_parts)
        q_own, q_keep, q_x, q_y = q_parts
        q_x, q_y = flipped(q_x, 2), flipped(q_y, 4)
        gkv, gkvt = finish_kv(kv_own, from_two, from_x)
        kv_parts = weight_partials(places, gkvt, flipped(gkvt, 1), x_local, x_other, block)
        w_blocks = (w_own, w_swapped, w_x, flipped(w_x, 1), w_y, flipped(w_y, 1))
        q_x, q_y, *rest = together(q_x, q_y, *kv_parts, *w_blocks)
        (kv_own, kv_keep, kv_x, kv_y), w_blocks = rest[:4], rest[4:]
        q_own, q_x, q_y = middle(q_own, q_keep, q_x, q_y)
        q_x, q_y = flipped(q_x, 2), flipped(q_y, 4)
        kv_x, kv_y = flipped(kv_x, 2), flipped(kv_y, 4)
        q_own, *q_pieces = quarters_of(z, q_own, q_x, q_y)
        q_pieces = crossed(q_pieces)
        kv_own, q_own = together(kv_own, q_own)
        kv_own, kv_x, kv_y = middle(kv_own, kv_keep, kv_x, kv_y)
        kv_x, kv_y = flipped(kv_x, 2), flipped(kv_y, 4)
        kv_x, kv_y, *q_pieces = together(kv_x, kv_y, *q_pieces)
        kv_own, *kv_pieces = quarters_of(z, kv_own, kv_x, kv_y)
        kv_own, w_x, w_y, *kv_pieces = together(kv_own, w_x, w_y, *kv_pieces)
        kv_pieces = crossed(kv_pieces)
        half = block // 2
        w_top, w_bottom = flipped(w_x[:half], 4), flipped(w_y[half:], 2)
        grad_in = input_grad(places, gq, gkv, w_blocks, 0)
        *kv_pieces, grad_in, w_top, w_bottom = together(*kv_pieces, grad_in, w_top, w_bottom)
        w_d = jnp.concatenate([w_top, w_bottom])
        mine = added([(q_own, *q_pieces), (kv_own, *kv_pieces)])
        pieces = crossed([mine] * 3)
        grad_in = input_grad(places, gq, gkv, (w_d, flipped(w_d, 1)), 6, grad_in)
        *pieces, grad_in = together(*pieces, grad_in)
        weight_sum = joined(z, (mine, *pieces), q_own.shape[0])
    else:
        from_two = lax.ppermute(kv_d2, "ctx", back(by_two))
        gkv, _ = finish_kv(kv_own, from_two, from_x)
        grad_qkv = jnp.concatenate([gq, gkv], axis=1)
        grad_in = nt_dot(grad_qkv, w_full).astype(bf16)
        partial = lax.dot_general(
            x_local, grad_qkv, (((0,), (0,)), ((), ())), preferred_element_type=f32
        )
        shard = lax.psum_scatter(partial, "ctx", scatter_dimension=0, tiled=True)
        weight_sum = lax.psum(shard, "dp").astype(bf16)
    return (gq[None], gkv[None], grad_in[None], weight_sum)


def solution(mesh):
    placed = (
        P("dp", "ctx", None),
        P("ctx", None),
        P("dp", "ctx", None),
        P("dp", "ctx", None),
        P("dp", "ctx", None),
        P("dp", None),
    )
    return jax.shard_map(
        per_device,
        mesh=mesh,
        in_specs=placed,
        out_specs=(
            P("dp", "ctx", None),
            P("dp", "ctx", None),
            P("dp", "ctx", None),
            P("ctx", None),
        ),
        check_vma=False,
    )
```

```python
import functools

import jax
import jax.numpy as jnp
from jax import lax
from jax.experimental import pallas as pl
from jax.experimental.pallas import tpu as pltpu
from jax.sharding import PartitionSpec as P

MOST = 1536
NEG_FILL = -1e30
LOG2E = 1.4426950408889634
KEY_STEP = 512
Q_STEP = 256


SMALL_VMEM = 4 * 2**20
VMEM = pl.BlockSpec(memory_space=pltpu.VMEM)


def nt_dot(a, b):
    return lax.dot_general(a, b, (((1,), (1,)), ((), ())), preferred_element_type=jnp.float32)


def nn_dot(a, b):
    return lax.dot_general(a, b, (((1,), (0,)), ((), ())), preferred_element_type=jnp.float32)


def attention_kernel(
    info_ref, q_ref, g_ref, own_ref, d2_ref, r_ref, x_ref,
    gq_ref, gqt_ref, own_out, d2_out, r_out, x_out,
    kv_scr, kt_scr, s_scr, dp_scr, acc_scr,
):
    rows = q_ref.shape[0]
    hd = kv_scr.shape[1] // 2
    heads = q_ref.shape[1] // hd
    wide = heads * Q_STEP
    scaling = hd ** (-0.5)
    index = info_ref[0]
    parity = lax.rem(index, 2)
    base = (index - 3) * rows
    r_off = pl.multiple_of((1 - parity) * 2 * rows, rows)
    x_off = pl.multiple_of(parity * 2 * rows, rows)
    kv_scr[pl.ds(r_off, rows), :] = r_ref[...]
    kv_scr[pl.ds(x_off, rows), :] = x_ref[...]
    kv_scr[rows : 2 * rows, :] = d2_ref[...]
    kv_scr[3 * rows :, :] = own_ref[...]
    for slot in range(4):
        part = slice(slot * rows, (slot + 1) * rows)
        kt_scr[:, part] = kv_scr[part, :hd].T
    acc_scr[...] = jnp.zeros_like(acc_scr)
    ends = []
    total = -base
    for j in range(1, info_ref.shape[0]):
        ends.append(total)
        total = total + info_ref[j]

    for tile in range(rows // Q_STEP):
        q_rows = slice(tile * Q_STEP, (tile + 1) * Q_STEP)
        first = 3 * rows + tile * Q_STEP
        q_pos = first + (lax.broadcasted_iota(jnp.int32, (1, wide), 1) & (Q_STEP - 1))
        doc_start = jnp.full((1, wide), ends[0], jnp.int32)
        least = ends[0]
        for end in ends[1:]:
            doc_start = jnp.where(q_pos >= end, end, doc_start)
            least = jnp.where(first >= end, end, least)
        q_cat = jnp.concatenate([q_ref[q_rows, h * hd : (h + 1) * hd] for h in range(heads)], axis=0)
        g_cat = jnp.concatenate([g_ref[q_rows, h * hd : (h + 1) * hd] for h in range(heads)], axis=0)
        begin = jnp.maximum(least, 0) // KEY_STEP
        stop = -(-(first + Q_STEP) // KEY_STEP)

        def scores_step(c, carried):
            top, norm, dot = carried
            at = pl.ds(pl.multiple_of(c * KEY_STEP, KEY_STEP), KEY_STEP)
            s = nt_dot(kv_scr[at, :hd], q_cat) * (scaling * LOG2E)
            k_pos = c * KEY_STEP + lax.broadcasted_iota(jnp.int32, (KEY_STEP, wide), 0)
            s = jnp.where((k_pos >= doc_start) & (k_pos <= q_pos), s, NEG_FILL)
            s_scr[at, :] = s
            dp = nt_dot(kv_scr[at, hd:], g_cat)
            dp_scr[at, :] = dp
            s = s.reshape(KEY_STEP // 8, 8, wide)
            above = jnp.maximum(top, jnp.max(s, axis=0))
            shrink = jnp.exp2(top - above)
            e = jnp.exp2(s - above[None])
            norm = norm * shrink + jnp.sum(e, axis=0)
            dot = dot * shrink + jnp.sum(e * dp.reshape(KEY_STEP // 8, 8, wide), axis=0)
            return above, norm, dot

        zero = jnp.zeros((8, wide), jnp.float32)
        tops, norms, dots = lax.fori_loop(
            begin, stop, scores_step, (jnp.full((8, wide), NEG_FILL, jnp.float32), zero, zero)
        )
        top = jnp.max(tops, axis=0, keepdims=True)
        shrink = jnp.exp2(tops - top)
        norm = jnp.sum(norms * shrink, axis=0, keepdims=True)
        delta = jnp.sum(dots * shrink, axis=0, keepdims=True) / norm
        lse = top + jnp.log2(norm)

        def grads_step(c, dq):
            at = pl.ds(pl.multiple_of(c * KEY_STEP, KEY_STEP), KEY_STEP)
            p = jnp.exp2(s_scr[at, :] - lse)
            ds_low = (p * (dp_scr[at, :] - delta)).astype(jnp.bfloat16)
            p_low = p.astype(jnp.bfloat16)
            acc_scr[at, :hd] += nn_dot(ds_low, q_cat)
            acc_scr[at, hd:] += nn_dot(p_low, g_cat)
            return dq + nn_dot(kt_scr[:, at], ds_low)

        dq = lax.fori_loop(begin, stop, grads_step, jnp.zeros((hd, wide), jnp.float32)) * scaling
        for h in range(heads):
            piece = dq[:, h * Q_STEP : (h + 1) * Q_STEP]
            gqt_ref[h * hd : (h + 1) * hd, q_rows] = piece.astype(jnp.bfloat16)
            gq_ref[q_rows, h * hd : (h + 1) * hd] = piece.T.astype(jnp.bfloat16)

    def put(out, at):
        out[:, :hd] = (acc_scr[at, :hd] * scaling).astype(out.dtype)
        out[:, hd:] = acc_scr[at, hd:].astype(out.dtype)

    put(r_out, pl.ds(r_off, rows))
    put(x_out, pl.ds(x_off, rows))
    put(d2_out, slice(rows, 2 * rows))
    put(own_out, slice(3 * rows, 4 * rows))


def attention(info, q, g, own, d2, r, x):
    rows, width = q.shape
    both = own.shape[1]
    hd = both // 2
    wide = width // hd * Q_STEP
    smem = pl.BlockSpec(memory_space=pltpu.SMEM)
    return pl.pallas_call(
        attention_kernel,
        name="attention",
        out_shape=(
            jax.ShapeDtypeStruct((rows, width), jnp.bfloat16),
            jax.ShapeDtypeStruct((width, rows), jnp.bfloat16),
            jax.ShapeDtypeStruct((rows, both), jnp.float32),
            jax.ShapeDtypeStruct((rows, both), jnp.float32),
            jax.ShapeDtypeStruct((rows, both), jnp.float32),
            jax.ShapeDtypeStruct((rows, both), jnp.bfloat16),
        ),
        in_specs=[smem] + [VMEM] * 6,
        out_specs=[VMEM] * 6,
        scratch_shapes=[
            pltpu.VMEM((4 * rows, both), jnp.bfloat16),
            pltpu.VMEM((hd, 4 * rows), jnp.bfloat16),
            pltpu.VMEM((4 * rows, wide), jnp.float32),
            pltpu.VMEM((4 * rows, wide), jnp.float32),
            pltpu.VMEM((4 * rows, both), jnp.float32),
        ],
        compiler_params=pltpu.CompilerParams(vmem_limit_bytes=30 * 2**20),
        cost_estimate=pl.CostEstimate(flops=12 * 10**9, bytes_accessed=6 * 2**20, transcendentals=4 * 2**20),
    )(info, q, g, own, d2, r, x)


def staged_kernel(*refs):
    count = len(refs) // 2
    for source, target in zip(refs[:count], refs[count:]):
        step = 64

        def body(start, source=source, target=target):
            target[pl.ds(start, step), :] = source[pl.ds(start, step), :]

        row_loop(source.shape[0], step, body)


def staged(*arrays):
    return pl.pallas_call(
        staged_kernel,
        name="staged",
        out_shape=[jax.ShapeDtypeStruct(a.shape, a.dtype) for a in arrays],
        in_specs=[VMEM] * len(arrays),
        out_specs=[VMEM] * len(arrays),
        compiler_params=pltpu.CompilerParams(vmem_limit_bytes=SMALL_VMEM),
        cost_estimate=pl.CostEstimate(flops=2**20, bytes_accessed=3 * 2**20, transcendentals=0),
    )(*arrays)


def weight_kernel(places, gt_ref, gt_other, x_ref, x_other, own_out, keep_out, to_x, to_y):
    k = pl.program_id(0)
    half = gt_ref.shape[0] // 2
    upper, lower = slice(0, half), slice(half, 2 * half)
    total = nn_dot(gt_ref[...], x_ref[...]) + nn_dot(gt_other[...], x_other[...])
    low = total.astype(jnp.bfloat16)

    @pl.when(k == 3)
    def _():
        own_out[...] = total

    @pl.when(k == 1)
    def _():
        to_x[upper, :] = low[upper, :]
        keep_out[lower, :] = low[lower, :]

    @pl.when(k == 2)
    def _():
        keep_out[upper, :] = low[upper, :]
        to_y[upper, :] = low[lower, :]

    @pl.when(k == 0)
    def _():
        to_x[lower, :] = low[upper, :]
        to_y[lower, :] = low[lower, :]


def weight_partials(places, gt, gt_other, x, x_other, block):
    cols, rows = gt.shape
    chips = x_other.shape[1] // block // 2
    strip = pl.BlockSpec((rows, block), lambda k, s: (0, (s[0] ^ s[2 + k]) * 2 + s[1]))
    return pl.pallas_call(
        weight_kernel,
        name="weight_partials",
        out_shape=[jax.ShapeDtypeStruct((cols, block), jnp.float32)]
        + [jax.ShapeDtypeStruct((cols, block), jnp.bfloat16)] * 3,
        grid_spec=pltpu.PrefetchScalarGridSpec(
            num_scalar_prefetch=1,
            grid=(chips,),
            in_specs=[VMEM] * 2 + [strip] * 2,
            out_specs=[VMEM] * 4,
        ),
        compiler_params=pltpu.CompilerParams(vmem_limit_bytes=12 * 2**20),
        cost_estimate=pl.CostEstimate(
            flops=4 * cols * rows * block * chips, bytes_accessed=8 * 2**20, transcendentals=0
        ),
    )(places, gt, gt_other, x, x_other)


def row_loop(rows, step, body):
    def turn(i, carried):
        body(pl.multiple_of(i * step, step))
        return carried

    lax.fori_loop(0, rows // step, turn, 0)


def middle_kernel(own_ref, keep_ref, from_x, from_y, own_out, next_x, next_y):
    f32 = jnp.float32
    half = own_ref.shape[0] // 2
    step = 32

    def body(at):
        top, low = pl.ds(at, step), pl.ds(half + at, step)
        own_out[top, :] = own_ref[top, :] + from_x[top, :].astype(f32)
        own_out[low, :] = own_ref[low, :] + from_y[top, :].astype(f32)
        next_y[top, :] = (keep_ref[top, :].astype(f32) + from_x[low, :].astype(f32)).astype(next_y.dtype)
        next_x[top, :] = (keep_ref[low, :].astype(f32) + from_y[low, :].astype(f32)).astype(next_x.dtype)

    row_loop(half, step, body)


def middle(own, keep, from_x, from_y):
    rows, cols = own.shape
    half = jax.ShapeDtypeStruct((rows // 2, cols), jnp.bfloat16)
    return pl.pallas_call(
        middle_kernel,
        name="middle",
        out_shape=[jax.ShapeDtypeStruct(own.shape, jnp.float32), half, half],
        in_specs=[VMEM] * 4,
        out_specs=[VMEM] * 3,
        compiler_params=pltpu.CompilerParams(vmem_limit_bytes=SMALL_VMEM),
        cost_estimate=pl.CostEstimate(flops=4 * rows * cols, bytes_accessed=2**21, transcendentals=0),
    )(own, keep, from_x, from_y)


def input_kernel(places, gq_ref, gkv_ref, *refs, count):
    out_ref = refs[-1]
    k = pl.program_id(0)
    q_cols = gq_ref.shape[1]
    for turn, w_ref in enumerate(refs[:count]):
        @pl.when(k == turn)
        def _(w_ref=w_ref):
            out_ref[...] = (
                nt_dot(gq_ref[...], w_ref[:, :q_cols]) + nt_dot(gkv_ref[...], w_ref[:, q_cols:])
            ).astype(out_ref.dtype)


def input_grad(places, gq, gkv, blocks, start, earlier=None):
    rows = gq.shape[0]
    block, cols = blocks[0].shape
    count = len(blocks)
    total = lax.axis_size("ctx") * block
    whole = lambda k, s: (0, 0)
    before = [] if earlier is None else [earlier]
    return pl.pallas_call(
        functools.partial(input_kernel, count=count),
        name="input_grad",
        out_shape=jax.ShapeDtypeStruct((rows, total), jnp.bfloat16),
        grid_spec=pltpu.PrefetchScalarGridSpec(
            num_scalar_prefetch=1,
            grid=(count,),
            in_specs=[pl.BlockSpec(gq.shape, whole), pl.BlockSpec(gkv.shape, whole)]
            + [pl.BlockSpec((block, cols), whole)] * count
            + [pl.BlockSpec(memory_space=pl.ANY)] * len(before),
            out_specs=pl.BlockSpec((rows, block), lambda k, s: (0, (s[0] * 2 + s[1]) ^ (start + k))),
        ),
        input_output_aliases={3 + count: 0} if before else {},
        compiler_params=pltpu.CompilerParams(vmem_limit_bytes=20 * 2**20),
        cost_estimate=pl.CostEstimate(
            flops=2 * rows * cols * block * count, bytes_accessed=11 * 2**20, transcendentals=0
        ),
    )(places, gq, gkv, *blocks, *before)


def finish_kernel(own_ref, two_ref, x_ref, out_ref, out_t_ref):
    step = 128

    def body(start):
        at = pl.ds(start, step)
        total = own_ref[at, :] + two_ref[at, :].astype(jnp.float32) + x_ref[at, :].astype(jnp.float32)
        out_ref[at, :] = total.astype(out_ref.dtype)
        out_t_ref[:, at] = total.T.astype(out_t_ref.dtype)

    row_loop(own_ref.shape[0], step, body)


def finish_kv(own, from_two, from_x):
    rows, cols = own.shape
    return pl.pallas_call(
        finish_kernel,
        name="finish_kv",
        out_shape=(
            jax.ShapeDtypeStruct((rows, cols), jnp.bfloat16),
            jax.ShapeDtypeStruct((cols, rows), jnp.bfloat16),
        ),
        in_specs=[VMEM] * 3,
        out_specs=[VMEM] * 2,
        compiler_params=pltpu.CompilerParams(vmem_limit_bytes=SMALL_VMEM),
        cost_estimate=pl.CostEstimate(flops=4 * rows * cols, bytes_accessed=2**21, transcendentals=0),
    )(own, from_two, from_x)


def quarters_kernel(z_ref, own_ref, x_ref, y_ref, mine_out, *outs):
    z = z_ref[0]
    quarter = mine_out.shape[0]
    step = 32
    for k, out in enumerate((mine_out, *outs)):
        place = z ^ k

        def body(start, place=place, out=out):
            at = pl.ds(pl.multiple_of(place * quarter + start, step), step)
            half = pl.ds(pl.multiple_of(lax.rem(place, 2) * quarter + start, step), step)
            add = jnp.where(place < 2, y_ref[half, :].astype(jnp.float32), x_ref[half, :].astype(jnp.float32))
            out[pl.ds(start, step), :] = (own_ref[at, :] + add).astype(out.dtype)

        row_loop(quarter, step, body)


def quarters_of(z, own, from_x, from_y):
    rows, cols = own.shape
    piece = (rows // 4, cols)
    return pl.pallas_call(
        quarters_kernel,
        name="quarters",
        out_shape=[jax.ShapeDtypeStruct(piece, jnp.float32)] + [jax.ShapeDtypeStruct(piece, jnp.bfloat16)] * 3,
        in_specs=[pl.BlockSpec(memory_space=pltpu.SMEM)] + [VMEM] * 3,
        out_specs=[VMEM] * 4,
        compiler_params=pltpu.CompilerParams(vmem_limit_bytes=SMALL_VMEM),
        cost_estimate=pl.CostEstimate(flops=4 * rows * cols, bytes_accessed=2**21, transcendentals=0),
    )(z, own, from_x, from_y)


def added_kernel(*refs):
    out_ref = refs[-1]
    first = 0
    step = 32
    for part in range(0, len(refs) - 1, 4):
        own = refs[part]

        def body(start, part=part, first=first):
            at = pl.ds(start, step)
            total = refs[part][at, :]
            for ref in refs[part + 1 : part + 4]:
                total = total + ref[at, :].astype(jnp.float32)
            out_ref[pl.ds(pl.multiple_of(first + start, step), step), :] = total.astype(out_ref.dtype)

        row_loop(own.shape[0], step, body)
        first += own.shape[0]


def added(parts):
    pieces = [piece for part in parts for piece in part]
    rows, cols = sum(part[0].shape[0] for part in parts), pieces[0].shape[1]
    return pl.pallas_call(
        added_kernel,
        name="added",
        out_shape=jax.ShapeDtypeStruct((rows, cols), jnp.bfloat16),
        in_specs=[VMEM] * len(pieces),
        out_specs=VMEM,
        compiler_params=pltpu.CompilerParams(vmem_limit_bytes=SMALL_VMEM),
        cost_estimate=pl.CostEstimate(flops=4 * rows * cols, bytes_accessed=2**20, transcendentals=0),
    )(*pieces)


def joined_kernel(z_ref, *refs, split):
    z = z_ref[0]
    *pieces, out_ref, scr = refs
    rest = pieces[0].shape[0] - split
    for k, piece in enumerate(pieces):
        place = z ^ k
        scr[pl.ds(pl.multiple_of(place * split, split), split), :] = piece[:split, :]
        scr[pl.ds(pl.multiple_of(4 * split + place * rest, rest), rest), :] = piece[split:, :]

    def body(start):
        at = pl.ds(start, 128)
        out_ref[:, at] = scr[at, :].T

    row_loop(scr.shape[0], 128, body)


def joined(z, pieces, split):
    rows, cols = pieces[0].shape
    return pl.pallas_call(
        functools.partial(joined_kernel, split=split),
        name="joined",
        out_shape=jax.ShapeDtypeStruct((cols, 4 * rows), jnp.bfloat16),
        in_specs=[pl.BlockSpec(memory_space=pltpu.SMEM)] + [VMEM] * 4,
        out_specs=VMEM,
        scratch_shapes=[pltpu.VMEM((4 * rows, cols), jnp.bfloat16)],
        compiler_params=pltpu.CompilerParams(vmem_limit_bytes=SMALL_VMEM),
        cost_estimate=pl.CostEstimate(flops=rows * cols, bytes_accessed=2**21, transcendentals=0),
    )(z, *pieces)


def flipped(array, bits, axis="ctx"):
    return lax.ppermute(array, axis, [(i, i ^ bits) for i in range(lax.axis_size(axis))])


def together(*arrays):
    return lax.optimization_barrier(arrays)


def per_device(inputs, qkv_weight, queries, keys_values, out_grad, lengths):
    f32, bf16 = jnp.float32, jnp.bfloat16
    size = lax.axis_size("ctx")
    planes = lax.axis_size("dp")
    index = lax.axis_index("ctx")
    rows = queries.shape[1]
    assert MOST == 3 * rows
    own = keys_values[0]

    def needed(source, target):
        first = target * rows
        earliest = max(first - (MOST - 1), 1 + MOST if first >= 1 + MOST else 0)
        return (source + 1) * rows > earliest

    by_two = [(i, i + 2) for i in range(size - 2) if needed(i, i + 2) or needed(i, (i + 2) ^ 1)]
    mixed = [(i, i + 1) for i in range(0, size, 2)]
    mixed += [(i, i + 3) for i in range(1, size - 3, 2) if needed(i, i + 3)]
    back = lambda pairs: [(b, a) for a, b in pairs]
    small = size == 8 and planes == 4
    block = qkv_weight.shape[0]
    x_local = inputs[0]

    d2 = lax.ppermute(own, "ctx", by_two)
    x = lax.ppermute(own, "ctx", mixed)
    w_swapped = flipped(qkv_weight, 1)
    places = jnp.stack([index // 2, index % 2, *map(jnp.int32, (3, 1, 2, 0))])
    info = jnp.concatenate([index.reshape(1), lengths[0]])
    q, g, near = staged(queries[0], out_grad[0], own)
    d2, x, w_swapped, places, info, q, g, near = together(d2, x, w_swapped, places, info, q, g, near)
    r = flipped(d2, 1)
    if small:
        w_own, x_in, r = lax.optimization_barrier((qkv_weight, x_local, r))
        w_x, w_y = flipped(w_own, 2), flipped(w_own, 4)
        x_other = flipped(x_in, 1)
    else:
        w_full = lax.all_gather(qkv_weight, "ctx", axis=0, tiled=True)

    grads = attention(info, q, g, near, d2, r, x)
    if small:
        *grads, x_other = together(*grads, x_other)
    gq, gqt, kv_own, kv_d2, kv_r, kv_x = grads
    kv_d2 = (kv_d2 + flipped(kv_r, 1)).astype(bf16)
    from_x = lax.ppermute(kv_x, "ctx", back(mixed))

    if small:
        z = lax.axis_index("dp").reshape(1)

        def crossed(pieces):
            return [flipped(piece, k + 1, "dp") for k, piece in enumerate(pieces)]

        gqt_other, kv_d2, w_x, w_y = together(flipped(gqt, 1), kv_d2, w_x, w_y)
        from_two = lax.ppermute(kv_d2, "ctx", back(by_two))
        q_parts = weight_partials(places, gqt, gqt_other, x_local, x_other, block)
        from_two, from_x, w_x, w_y, *q_parts = together(from_two, from_x, w_x, w_y, *q_parts)
        q_own, q_keep, q_x, q_y = q_parts
        q_x, q_y = flipped(q_x, 2), flipped(q_y, 4)
        gkv, gkvt = finish_kv(kv_own, from_two, from_x)
        kv_parts = weight_partials(places, gkvt, flipped(gkvt, 1), x_local, x_other, block)
        w_blocks = (w_own, w_swapped, w_x, flipped(w_x, 1), w_y, flipped(w_y, 1))
        q_x, q_y, *rest = together(q_x, q_y, *kv_parts, *w_blocks)
        (kv_own, kv_keep, kv_x, kv_y), w_blocks = rest[:4], rest[4:]
        q_own, q_x, q_y = middle(q_own, q_keep, q_x, q_y)
        q_x, q_y = flipped(q_x, 2), flipped(q_y, 4)
        kv_x, kv_y = flipped(kv_x, 2), flipped(kv_y, 4)
        q_own, *q_pieces = quarters_of(z, q_own, q_x, q_y)
        q_pieces = crossed(q_pieces)
        kv_own, q_own = together(kv_own, q_own)
        kv_own, kv_x, kv_y = middle(kv_own, kv_keep, kv_x, kv_y)
        kv_x, kv_y = flipped(kv_x, 2), flipped(kv_y, 4)
        kv_x, kv_y, *q_pieces = together(kv_x, kv_y, *q_pieces)
        kv_own, *kv_pieces = quarters_of(z, kv_own, kv_x, kv_y)
        kv_own, w_x, w_y, *kv_pieces = together(kv_own, w_x, w_y, *kv_pieces)
        kv_pieces = crossed(kv_pieces)
        half = block // 2
        w_top, w_bottom = flipped(w_x[:half], 4), flipped(w_y[half:], 2)
        grad_in = input_grad(places, gq, gkv, w_blocks, 0)
        *kv_pieces, grad_in, w_top, w_bottom = together(*kv_pieces, grad_in, w_top, w_bottom)
        w_d = jnp.concatenate([w_top, w_bottom])
        mine = added([(q_own, *q_pieces), (kv_own, *kv_pieces)])
        pieces = crossed([mine] * 3)
        grad_in = input_grad(places, gq, gkv, (w_d, flipped(w_d, 1)), 6, grad_in)
        *pieces, grad_in = together(*pieces, grad_in)
        weight_sum = joined(z, (mine, *pieces), q_own.shape[0])
    else:
        from_two = lax.ppermute(kv_d2, "ctx", back(by_two))
        gkv, _ = finish_kv(kv_own, from_two, from_x)
        grad_qkv = jnp.concatenate([gq, gkv], axis=1)
        grad_in = nt_dot(grad_qkv, w_full).astype(bf16)
        partial = lax.dot_general(
            x_local, grad_qkv, (((0,), (0,)), ((), ())), preferred_element_type=f32
        )
        shard = lax.psum_scatter(partial, "ctx", scatter_dimension=0, tiled=True)
        weight_sum = lax.psum(shard, "dp").astype(bf16)
    return (gq[None], gkv[None], grad_in[None], weight_sum)


def solution(mesh):
    placed = (
        P("dp", "ctx", None),
        P("ctx", None),
        P("dp", "ctx", None),
        P("dp", "ctx", None),
        P("dp", "ctx", None),
        P("dp", None),
    )
    return jax.shard_map(
        per_device,
        mesh=mesh,
        in_specs=placed,
        out_specs=(
            P("dp", "ctx", None),
            P("dp", "ctx", None),
            P("dp", "ctx", None),
            P("ctx", None),
        ),
        check_vma=False,
    )
```

```python
import functools

import jax
import jax.numpy as jnp
from jax import lax
from jax.experimental import pallas as pl
from jax.experimental.pallas import tpu as pltpu
from jax.sharding import PartitionSpec as P

MOST = 1536
NEG_FILL = -1e30
LOG2E = 1.4426950408889634
KEY_STEP = 512
Q_STEP = 256


SMALL_VMEM = 2 * 2**20
VMEM = pl.BlockSpec(memory_space=pltpu.VMEM)


def nt_dot(a, b):
    return lax.dot_general(a, b, (((1,), (1,)), ((), ())), preferred_element_type=jnp.float32)


def nn_dot(a, b):
    return lax.dot_general(a, b, (((1,), (0,)), ((), ())), preferred_element_type=jnp.float32)


def attention_kernel(
    info_ref, q_ref, g_ref, own_ref, d2_ref, r_ref, x_ref,
    gq_ref, gqt_ref, own_out, d2_out, r_out, x_out,
    kv_scr, kt_scr, s_scr, dp_scr, acc_scr,
):
    rows = q_ref.shape[0]
    hd = kv_scr.shape[1] // 2
    heads = q_ref.shape[1] // hd
    wide = heads * Q_STEP
    scaling = hd ** (-0.5)
    index = info_ref[0]
    parity = lax.rem(index, 2)
    base = (index - 3) * rows
    r_off = pl.multiple_of((1 - parity) * 2 * rows, rows)
    x_off = pl.multiple_of(parity * 2 * rows, rows)
    kv_scr[pl.ds(r_off, rows), :] = r_ref[...]
    kv_scr[pl.ds(x_off, rows), :] = x_ref[...]
    kv_scr[rows : 2 * rows, :] = d2_ref[...]
    kv_scr[3 * rows :, :] = own_ref[...]
    for slot in range(4):
        part = slice(slot * rows, (slot + 1) * rows)
        kt_scr[:, part] = kv_scr[part, :hd].T
    acc_scr[...] = jnp.zeros_like(acc_scr)
    ends = []
    total = -base
    for j in range(1, info_ref.shape[0]):
        ends.append(total)
        total = total + info_ref[j]

    for tile in range(rows // Q_STEP):
        q_rows = slice(tile * Q_STEP, (tile + 1) * Q_STEP)
        first = 3 * rows + tile * Q_STEP
        q_pos = first + (lax.broadcasted_iota(jnp.int32, (1, wide), 1) & (Q_STEP - 1))
        doc_start = jnp.full((1, wide), ends[0], jnp.int32)
        least = ends[0]
        for end in ends[1:]:
            doc_start = jnp.where(q_pos >= end, end, doc_start)
            least = jnp.where(first >= end, end, least)
        q_cat = jnp.concatenate([q_ref[q_rows, h * hd : (h + 1) * hd] for h in range(heads)], axis=0)
        g_cat = jnp.concatenate([g_ref[q_rows, h * hd : (h + 1) * hd] for h in range(heads)], axis=0)
        begin = jnp.maximum(least, 0) // KEY_STEP
        stop = -(-(first + Q_STEP) // KEY_STEP)

        def scores_step(c, carried):
            top, norm, dot = carried
            at = pl.ds(pl.multiple_of(c * KEY_STEP, KEY_STEP), KEY_STEP)
            s = nt_dot(kv_scr[at, :hd], q_cat) * (scaling * LOG2E)
            k_pos = c * KEY_STEP + lax.broadcasted_iota(jnp.int32, (KEY_STEP, wide), 0)
            s = jnp.where((k_pos >= doc_start) & (k_pos <= q_pos), s, NEG_FILL)
            s_scr[at, :] = s
            dp = nt_dot(kv_scr[at, hd:], g_cat)
            dp_scr[at, :] = dp
            s = s.reshape(KEY_STEP // 8, 8, wide)
            above = jnp.maximum(top, jnp.max(s, axis=0))
            shrink = jnp.exp2(top - above)
            e = jnp.exp2(s - above[None])
            norm = norm * shrink + jnp.sum(e, axis=0)
            dot = dot * shrink + jnp.sum(e * dp.reshape(KEY_STEP // 8, 8, wide), axis=0)
            return above, norm, dot

        zero = jnp.zeros((8, wide), jnp.float32)
        tops, norms, dots = lax.fori_loop(
            begin, stop, scores_step, (jnp.full((8, wide), NEG_FILL, jnp.float32), zero, zero)
        )
        top = jnp.max(tops, axis=0, keepdims=True)
        shrink = jnp.exp2(tops - top)
        norm = jnp.sum(norms * shrink, axis=0, keepdims=True)
        delta = jnp.sum(dots * shrink, axis=0, keepdims=True) / norm
        lse = top + jnp.log2(norm)

        def grads_step(c, dq):
            at = pl.ds(pl.multiple_of(c * KEY_STEP, KEY_STEP), KEY_STEP)
            p = jnp.exp2(s_scr[at, :] - lse)
            ds_low = (p * (dp_scr[at, :] - delta)).astype(jnp.bfloat16)
            p_low = p.astype(jnp.bfloat16)
            acc_scr[at, :hd] += nn_dot(ds_low, q_cat)
            acc_scr[at, hd:] += nn_dot(p_low, g_cat)
            return dq + nn_dot(kt_scr[:, at], ds_low)

        dq = lax.fori_loop(begin, stop, grads_step, jnp.zeros((hd, wide), jnp.float32)) * scaling
        for h in range(heads):
            piece = dq[:, h * Q_STEP : (h + 1) * Q_STEP]
            gqt_ref[h * hd : (h + 1) * hd, q_rows] = piece.astype(jnp.bfloat16)
            gq_ref[q_rows, h * hd : (h + 1) * hd] = piece.T.astype(jnp.bfloat16)

    def put(out, at):
        out[:, :hd] = (acc_scr[at, :hd] * scaling).astype(out.dtype)
        out[:, hd:] = acc_scr[at, hd:].astype(out.dtype)

    put(r_out, pl.ds(r_off, rows))
    put(x_out, pl.ds(x_off, rows))
    put(d2_out, slice(rows, 2 * rows))
    put(own_out, slice(3 * rows, 4 * rows))


def attention(info, q, g, own, d2, r, x):
    rows, width = q.shape
    both = own.shape[1]
    hd = both // 2
    wide = width // hd * Q_STEP
    smem = pl.BlockSpec(memory_space=pltpu.SMEM)
    return pl.pallas_call(
        attention_kernel,
        name="attention",
        out_shape=(
            jax.ShapeDtypeStruct((rows, width), jnp.bfloat16),
            jax.ShapeDtypeStruct((width, rows), jnp.bfloat16),
            jax.ShapeDtypeStruct((rows, both), jnp.float32),
            jax.ShapeDtypeStruct((rows, both), jnp.float32),
            jax.ShapeDtypeStruct((rows, both), jnp.float32),
            jax.ShapeDtypeStruct((rows, both), jnp.bfloat16),
        ),
        in_specs=[smem] + [VMEM] * 6,
        out_specs=[VMEM] * 6,
        scratch_shapes=[
            pltpu.VMEM((4 * rows, both), jnp.bfloat16),
            pltpu.VMEM((hd, 4 * rows), jnp.bfloat16),
            pltpu.VMEM((4 * rows, wide), jnp.float32),
            pltpu.VMEM((4 * rows, wide), jnp.float32),
            pltpu.VMEM((4 * rows, both), jnp.float32),
        ],
        compiler_params=pltpu.CompilerParams(vmem_limit_bytes=28 * 2**20),
        cost_estimate=pl.CostEstimate(flops=12 * 10**9, bytes_accessed=6 * 2**20, transcendentals=4 * 2**20),
    )(info, q, g, own, d2, r, x)


def staged_kernel(*refs):
    count = len(refs) // 2
    for source, target in zip(refs[:count], refs[count:]):
        step = 64

        def body(start, source=source, target=target):
            target[pl.ds(start, step), :] = source[pl.ds(start, step), :]

        row_loop(source.shape[0], step, body)


def staged(*arrays):
    return pl.pallas_call(
        staged_kernel,
        name="staged",
        out_shape=[jax.ShapeDtypeStruct(a.shape, a.dtype) for a in arrays],
        in_specs=[VMEM] * len(arrays),
        out_specs=[VMEM] * len(arrays),
        compiler_params=pltpu.CompilerParams(vmem_limit_bytes=SMALL_VMEM),
        cost_estimate=pl.CostEstimate(flops=2**20, bytes_accessed=3 * 2**20, transcendentals=0),
    )(*arrays)


def weight_kernel(places, gt_ref, gt_other, x_ref, x_other, own_out, keep_out, to_x, to_y):
    k = pl.program_id(0)
    half = gt_ref.shape[0] // 2
    upper, lower = slice(0, half), slice(half, 2 * half)
    total = nn_dot(gt_ref[...], x_ref[...]) + nn_dot(gt_other[...], x_other[...])
    low = total.astype(jnp.bfloat16)

    @pl.when(k == 3)
    def _():
        own_out[...] = total

    @pl.when(k == 1)
    def _():
        to_x[upper, :] = low[upper, :]
        keep_out[lower, :] = low[lower, :]

    @pl.when(k == 2)
    def _():
        keep_out[upper, :] = low[upper, :]
        to_y[upper, :] = low[lower, :]

    @pl.when(k == 0)
    def _():
        to_x[lower, :] = low[upper, :]
        to_y[lower, :] = low[lower, :]


def weight_partials(places, gt, gt_other, x, x_other, block):
    cols, rows = gt.shape
    chips = x_other.shape[1] // block // 2
    strip = pl.BlockSpec((rows, block), lambda k, s: (0, (s[0] ^ s[2 + k]) * 2 + s[1]))
    return pl.pallas_call(
        weight_kernel,
        name="weight_partials",
        out_shape=[jax.ShapeDtypeStruct((cols, block), jnp.float32)]
        + [jax.ShapeDtypeStruct((cols, block), jnp.bfloat16)] * 3,
        grid_spec=pltpu.PrefetchScalarGridSpec(
            num_scalar_prefetch=1,
            grid=(chips,),
            in_specs=[VMEM] * 2 + [strip] * 2,
            out_specs=[VMEM] * 4,
        ),
        compiler_params=pltpu.CompilerParams(vmem_limit_bytes=9 * 2**20),
        cost_estimate=pl.CostEstimate(
            flops=4 * cols * rows * block * chips, bytes_accessed=8 * 2**20, transcendentals=0
        ),
    )(places, gt, gt_other, x, x_other)


def row_loop(rows, step, body):
    def turn(i, carried):
        body(pl.multiple_of(i * step, step))
        return carried

    lax.fori_loop(0, rows // step, turn, 0)


def middle_kernel(own_ref, keep_ref, from_x, from_y, own_out, next_x, next_y):
    f32 = jnp.float32
    half = own_ref.shape[0] // 2
    step = 32

    def body(at):
        top, low = pl.ds(at, step), pl.ds(half + at, step)
        own_out[top, :] = own_ref[top, :] + from_x[top, :].astype(f32)
        own_out[low, :] = own_ref[low, :] + from_y[top, :].astype(f32)
        next_y[top, :] = (keep_ref[top, :].astype(f32) + from_x[low, :].astype(f32)).astype(next_y.dtype)
        next_x[top, :] = (keep_ref[low, :].astype(f32) + from_y[low, :].astype(f32)).astype(next_x.dtype)

    row_loop(half, step, body)


def middle(own, keep, from_x, from_y):
    rows, cols = own.shape
    half = jax.ShapeDtypeStruct((rows // 2, cols), jnp.bfloat16)
    return pl.pallas_call(
        middle_kernel,
        name="middle",
        out_shape=[jax.ShapeDtypeStruct(own.shape, jnp.float32), half, half],
        in_specs=[VMEM] * 4,
        out_specs=[VMEM] * 3,
        compiler_params=pltpu.CompilerParams(vmem_limit_bytes=SMALL_VMEM),
        cost_estimate=pl.CostEstimate(flops=4 * rows * cols, bytes_accessed=2**21, transcendentals=0),
    )(own, keep, from_x, from_y)


def input_kernel(places, gq_ref, gkv_ref, *refs, count):
    out_ref = refs[-1]
    k = pl.program_id(0)
    q_cols = gq_ref.shape[1]
    for turn, w_ref in enumerate(refs[:count]):
        @pl.when(k == turn)
        def _(w_ref=w_ref):
            out_ref[...] = (
                nt_dot(gq_ref[...], w_ref[:, :q_cols]) + nt_dot(gkv_ref[...], w_ref[:, q_cols:])
            ).astype(out_ref.dtype)


def input_grad(places, gq, gkv, blocks, start, earlier=None):
    rows = gq.shape[0]
    block, cols = blocks[0].shape
    count = len(blocks)
    total = lax.axis_size("ctx") * block
    whole = lambda k, s: (0, 0)
    before = [] if earlier is None else [earlier]
    return pl.pallas_call(
        functools.partial(input_kernel, count=count),
        name="input_grad",
        out_shape=jax.ShapeDtypeStruct((rows, total), jnp.bfloat16),
        grid_spec=pltpu.PrefetchScalarGridSpec(
            num_scalar_prefetch=1,
            grid=(count,),
            in_specs=[pl.BlockSpec(gq.shape, whole), pl.BlockSpec(gkv.shape, whole)]
            + [pl.BlockSpec((block, cols), whole)] * count
            + [pl.BlockSpec(memory_space=pl.ANY)] * len(before),
            out_specs=pl.BlockSpec((rows, block), lambda k, s: (0, (s[0] * 2 + s[1]) ^ (start + k))),
        ),
        input_output_aliases={3 + count: 0} if before else {},
        compiler_params=pltpu.CompilerParams(vmem_limit_bytes=20 * 2**20),
        cost_estimate=pl.CostEstimate(
            flops=2 * rows * cols * block * count, bytes_accessed=11 * 2**20, transcendentals=0
        ),
    )(places, gq, gkv, *blocks, *before)


def finish_kernel(own_ref, two_ref, x_ref, out_ref, out_t_ref):
    step = 128

    def body(start):
        at = pl.ds(start, step)
        total = own_ref[at, :] + two_ref[at, :].astype(jnp.float32) + x_ref[at, :].astype(jnp.float32)
        out_ref[at, :] = total.astype(out_ref.dtype)
        out_t_ref[:, at] = total.T.astype(out_t_ref.dtype)

    row_loop(own_ref.shape[0], step, body)


def finish_kv(own, from_two, from_x):
    rows, cols = own.shape
    return pl.pallas_call(
        finish_kernel,
        name="finish_kv",
        out_shape=(
            jax.ShapeDtypeStruct((rows, cols), jnp.bfloat16),
            jax.ShapeDtypeStruct((cols, rows), jnp.bfloat16),
        ),
        in_specs=[VMEM] * 3,
        out_specs=[VMEM] * 2,
        compiler_params=pltpu.CompilerParams(vmem_limit_bytes=SMALL_VMEM),
        cost_estimate=pl.CostEstimate(flops=4 * rows * cols, bytes_accessed=2**21, transcendentals=0),
    )(own, from_two, from_x)


def quarters_kernel(z_ref, own_ref, x_ref, y_ref, mine_out, *outs):
    z = z_ref[0]
    quarter = mine_out.shape[0]
    step = 32
    for k, out in enumerate((mine_out, *outs)):
        place = z ^ k

        def body(start, place=place, out=out):
            at = pl.ds(pl.multiple_of(place * quarter + start, step), step)
            half = pl.ds(pl.multiple_of(lax.rem(place, 2) * quarter + start, step), step)
            add = jnp.where(place < 2, y_ref[half, :].astype(jnp.float32), x_ref[half, :].astype(jnp.float32))
            out[pl.ds(start, step), :] = (own_ref[at, :] + add).astype(out.dtype)

        row_loop(quarter, step, body)


def quarters_of(z, own, from_x, from_y):
    rows, cols = own.shape
    piece = (rows // 4, cols)
    return pl.pallas_call(
        quarters_kernel,
        name="quarters",
        out_shape=[jax.ShapeDtypeStruct(piece, jnp.float32)] + [jax.ShapeDtypeStruct(piece, jnp.bfloat16)] * 3,
        in_specs=[pl.BlockSpec(memory_space=pltpu.SMEM)] + [VMEM] * 3,
        out_specs=[VMEM] * 4,
        compiler_params=pltpu.CompilerParams(vmem_limit_bytes=SMALL_VMEM),
        cost_estimate=pl.CostEstimate(flops=4 * rows * cols, bytes_accessed=2**21, transcendentals=0),
    )(z, own, from_x, from_y)


def added_kernel(*refs):
    out_ref = refs[-1]
    first = 0
    step = 32
    for part in range(0, len(refs) - 1, 4):
        own = refs[part]

        def body(start, part=part, first=first):
            at = pl.ds(start, step)
            total = refs[part][at, :]
            for ref in refs[part + 1 : part + 4]:
                total = total + ref[at, :].astype(jnp.float32)
            out_ref[pl.ds(pl.multiple_of(first + start, step), step), :] = total.astype(out_ref.dtype)

        row_loop(own.shape[0], step, body)
        first += own.shape[0]


def added(parts):
    pieces = [piece for part in parts for piece in part]
    rows, cols = sum(part[0].shape[0] for part in parts), pieces[0].shape[1]
    return pl.pallas_call(
        added_kernel,
        name="added",
        out_shape=jax.ShapeDtypeStruct((rows, cols), jnp.bfloat16),
        in_specs=[VMEM] * len(pieces),
        out_specs=VMEM,
        compiler_params=pltpu.CompilerParams(vmem_limit_bytes=SMALL_VMEM),
        cost_estimate=pl.CostEstimate(flops=4 * rows * cols, bytes_accessed=2**20, transcendentals=0),
    )(*pieces)


def joined_kernel(z_ref, *refs, split):
    z = z_ref[0]
    *pieces, out_ref, scr = refs
    rest = pieces[0].shape[0] - split
    for k, piece in enumerate(pieces):
        place = z ^ k
        scr[pl.ds(pl.multiple_of(place * split, split), split), :] = piece[:split, :]
        scr[pl.ds(pl.multiple_of(4 * split + place * rest, rest), rest), :] = piece[split:, :]

    def body(start):
        at = pl.ds(start, 128)
        out_ref[:, at] = scr[at, :].T

    row_loop(scr.shape[0], 128, body)


def joined(z, pieces, split):
    rows, cols = pieces[0].shape
    return pl.pallas_call(
        functools.partial(joined_kernel, split=split),
        name="joined",
        out_shape=jax.ShapeDtypeStruct((cols, 4 * rows), jnp.bfloat16),
        in_specs=[pl.BlockSpec(memory_space=pltpu.SMEM)] + [VMEM] * 4,
        out_specs=VMEM,
        scratch_shapes=[pltpu.VMEM((4 * rows, cols), jnp.bfloat16)],
        compiler_params=pltpu.CompilerParams(vmem_limit_bytes=SMALL_VMEM),
        cost_estimate=pl.CostEstimate(flops=rows * cols, bytes_accessed=2**21, transcendentals=0),
    )(z, *pieces)


def flipped(array, bits, axis="ctx"):
    return lax.ppermute(array, axis, [(i, i ^ bits) for i in range(lax.axis_size(axis))])


def together(*arrays):
    return lax.optimization_barrier(arrays)


def per_device(inputs, qkv_weight, queries, keys_values, out_grad, lengths):
    f32, bf16 = jnp.float32, jnp.bfloat16
    size = lax.axis_size("ctx")
    planes = lax.axis_size("dp")
    index = lax.axis_index("ctx")
    rows = queries.shape[1]
    assert MOST == 3 * rows
    own = keys_values[0]

    def needed(source, target):
        first = target * rows
        earliest = max(first - (MOST - 1), 1 + MOST if first >= 1 + MOST else 0)
        return (source + 1) * rows > earliest

    by_two = [(i, i + 2) for i in range(size - 2) if needed(i, i + 2) or needed(i, (i + 2) ^ 1)]
    mixed = [(i, i + 1) for i in range(0, size, 2)]
    mixed += [(i, i + 3) for i in range(1, size - 3, 2) if needed(i, i + 3)]
    back = lambda pairs: [(b, a) for a, b in pairs]
    small = size == 8 and planes == 4
    block = qkv_weight.shape[0]
    x_local = inputs[0]

    d2 = lax.ppermute(own, "ctx", by_two)
    x = lax.ppermute(own, "ctx", mixed)
    w_swapped = flipped(qkv_weight, 1)
    places = jnp.stack([index // 2, index % 2, *map(jnp.int32, (3, 1, 2, 0))])
    info = jnp.concatenate([index.reshape(1), lengths[0]])
    q, g, near = staged(queries[0], out_grad[0], own)
    d2, x, w_swapped, places, info, q, g, near = together(d2, x, w_swapped, places, info, q, g, near)
    r = flipped(d2, 1)
    if small:
        w_own, x_in, r = lax.optimization_barrier((qkv_weight, x_local, r))
        w_x, w_y = flipped(w_own, 2), flipped(w_own, 4)
        x_other = flipped(x_in, 1)
    else:
        w_full = lax.all_gather(qkv_weight, "ctx", axis=0, tiled=True)

    grads = attention(info, q, g, near, d2, r, x)
    if small:
        *grads, x_other = together(*grads, x_other)
    gq, gqt, kv_own, kv_d2, kv_r, kv_x = grads
    kv_d2 = (kv_d2 + flipped(kv_r, 1)).astype(bf16)
    from_x = lax.ppermute(kv_x, "ctx", back(mixed))

    if small:
        z = lax.axis_index("dp").reshape(1)

        def crossed(pieces):
            return [flipped(piece, k + 1, "dp") for k, piece in enumerate(pieces)]

        gqt_other, kv_d2, w_x, w_y = together(flipped(gqt, 1), kv_d2, w_x, w_y)
        from_two = lax.ppermute(kv_d2, "ctx", back(by_two))
        q_parts = weight_partials(places, gqt, gqt_other, x_local, x_other, block)
        from_two, from_x, w_x, w_y, *q_parts = together(from_two, from_x, w_x, w_y, *q_parts)
        q_own, q_keep, q_x, q_y = q_parts
        q_x, q_y = flipped(q_x, 2), flipped(q_y, 4)
        gkv, gkvt = finish_kv(kv_own, from_two, from_x)
        kv_parts = weight_partials(places, gkvt, flipped(gkvt, 1), x_local, x_other, block)
        w_blocks = (w_own, w_swapped, w_x, flipped(w_x, 1), w_y, flipped(w_y, 1))
        q_x, q_y, *rest = together(q_x, q_y, *kv_parts, *w_blocks)
        (kv_own, kv_keep, kv_x, kv_y), w_blocks = rest[:4], rest[4:]
        q_own, q_x, q_y = middle(q_own, q_keep, q_x, q_y)
        q_x, q_y = flipped(q_x, 2), flipped(q_y, 4)
        kv_x, kv_y = flipped(kv_x, 2), flipped(kv_y, 4)
        q_own, *q_pieces = quarters_of(z, q_own, q_x, q_y)
        q_pieces = crossed(q_pieces)
        kv_own, q_own = together(kv_own, q_own)
        kv_own, kv_x, kv_y = middle(kv_own, kv_keep, kv_x, kv_y)
        kv_x, kv_y = flipped(kv_x, 2), flipped(kv_y, 4)
        kv_x, kv_y, *q_pieces = together(kv_x, kv_y, *q_pieces)
        kv_own, *kv_pieces = quarters_of(z, kv_own, kv_x, kv_y)
        kv_own, w_x, w_y, *kv_pieces = together(kv_own, w_x, w_y, *kv_pieces)
        kv_pieces = crossed(kv_pieces)
        half = block // 2
        w_top, w_bottom = flipped(w_x[:half], 4), flipped(w_y[half:], 2)
        grad_in = input_grad(places, gq, gkv, w_blocks, 0)
        *kv_pieces, grad_in, w_top, w_bottom = together(*kv_pieces, grad_in, w_top, w_bottom)
        w_d = jnp.concatenate([w_top, w_bottom])
        mine = added([(q_own, *q_pieces), (kv_own, *kv_pieces)])
        pieces = crossed([mine] * 3)
        grad_in = input_grad(places, gq, gkv, (w_d, flipped(w_d, 1)), 6, grad_in)
        *pieces, grad_in = together(*pieces, grad_in)
        weight_sum = joined(z, (mine, *pieces), q_own.shape[0])
    else:
        from_two = lax.ppermute(kv_d2, "ctx", back(by_two))
        gkv, _ = finish_kv(kv_own, from_two, from_x)
        grad_qkv = jnp.concatenate([gq, gkv], axis=1)
        grad_in = nt_dot(grad_qkv, w_full).astype(bf16)
        partial = lax.dot_general(
            x_local, grad_qkv, (((0,), (0,)), ((), ())), preferred_element_type=f32
        )
        shard = lax.psum_scatter(partial, "ctx", scatter_dimension=0, tiled=True)
        weight_sum = lax.psum(shard, "dp").astype(bf16)
    return (gq[None], gkv[None], grad_in[None], weight_sum)


def solution(mesh):
    placed = (
        P("dp", "ctx", None),
        P("ctx", None),
        P("dp", "ctx", None),
        P("dp", "ctx", None),
        P("dp", "ctx", None),
        P("dp", None),
    )
    return jax.shard_map(
        per_device,
        mesh=mesh,
        in_specs=placed,
        out_specs=(
            P("dp", "ctx", None),
            P("dp", "ctx", None),
            P("dp", "ctx", None),
            P("ctx", None),
        ),
        check_vma=False,
    )
```
